512 devices in a mesh: dp: 16 (over x, y_lo, core), owner: 32 (over y_hi, z).
Axes of the slice: x: 4, y: 8 (y_hi: 4, y_lo: 2; y = y_hi * 2 + y_lo), z: 8, core: 2. Of those that a mesh axis runs over, the one named last changes fastest.
Arguments:
- train_act: bfloat16 [2048, 4096], P('dp', 'owner')
- train_grad: bfloat16 [2048, 10240], P('dp', 'owner')
- query_act: bfloat16 [16, 4096], P(None, 'owner'), may hold values from -6 to 6
- query_grad: bfloat16 [16, 10240], P(None, 'owner'), may hold values from -6 to 6
- query_of: int32 [16], replicated, may hold values from 0 to 7, as said below
- counts: int32 [16], replicated, may hold values from 1 to 128, 1536 in all
- eig_act: bfloat16 [4096, 4096], P(None, 'owner')
- eig_grad: bfloat16 [10240, 10240], P('dp', 'owner')
Outputs:
- scores: float32 [8, 2048], P(None, ('dp', 'owner'))
- corrections: float32 [4096, 10240], P('dp', 'owner')
The draws below stay inside these ranges and needn't reach their ends.
Inputs may be any that keep to these rules, and one draw needn't show every extreme that they name: `query_of`: each of the 8 queries owns exactly 2 rows.
All inputs are finite; a program needn't handle non-finite values.
Results may differ from the reference program's by a relative error of at most 0.019.
Values may be sent and summed in bfloat16 or wider, within the bound.
A program may use at most 64 MiB of HBM per device.

```python
import math
import jax
import jax.numpy as jnp
import numpy as np
from jax import lax

D = 4096
FF = 10240
TOK_DEV = 128
QUERIES = 8
QTOK = 2
TOKENS = 2048
QROWS = 16
N_DP = 16


def row_scaled(key, height, breadth, low, high):
    noise = jax.random.normal(jax.random.fold_in(key, 11), (height, breadth), jnp.float32)
    spread = jnp.exp(jax.random.uniform(jax.random.fold_in(key, 12), (height, 1), jnp.float32, math.log(low), math.log(high)))
    return noise * spread


def column_scaled(key, order_size):
    noise = jax.random.normal(jax.random.fold_in(key, 13), (order_size, order_size), jnp.float32)
    spread = jnp.exp(jax.random.uniform(jax.random.fold_in(key, 14), (1, order_size), jnp.float32, math.log(0.5), math.log(2.0)))
    return noise * spread / math.sqrt(order_size)


def draw_train_act(key, part):
    key = jax.random.fold_in(key, 1)
    return row_scaled(key, TOKENS, D, 0.3, 3.0).astype(jnp.bfloat16)


def draw_train_grad(key, part):
    key = jax.random.fold_in(key, 2)
    return row_scaled(key, TOKENS, FF, 0.3, 3.0).astype(jnp.bfloat16)


def draw_eig_act(key, part):
    key = jax.random.fold_in(key, 3)
    return column_scaled(key, D).astype(jnp.bfloat16)


def draw_eig_grad(key, part):
    key = jax.random.fold_in(key, 4)
    return column_scaled(key, FF).astype(jnp.bfloat16)


def draw_query_of(key, part):
    key = jax.random.fold_in(key, 5)
    return (jax.random.permutation(key, QROWS) // QTOK).astype(jnp.int32)


def block_levels(rng, shape, split, low, largest):
    factor_of = 1.0
    for dim, parts in split:
        steps = jax.random.uniform(jax.random.fold_in(jax.random.fold_in(rng, 6), dim), (parts,), jnp.float32, low / len(split), largest / len(split))
        factor_of = factor_of * jnp.repeat(jnp.exp(steps), shape[dim] // parts).reshape((-1,) + (1,) * (len(shape) - 1 - dim))
    return factor_of


def profile(amount, total, reach, skew):
    portions = [(1 << 20) // math.isqrt(rank ** skew) + 1 for rank in range(2, amount + 1)]
    rest, given = total - reach - (amount - 1), [1] * (amount - 1)
    while rest > 0:
        movable = [i for i in range(amount - 1) if given[i] < reach]
        pool, left = sum([portions[i] for i in movable]), rest
        for i in movable:
            more = min(reach - given[i], max(1, left * portions[i] // pool), rest)
            given[i] = given[i] + more
            rest = rest - more
    return np.array([reach] + given)


def uneven_parts(key, number_of, total, reach, slope):
    if number_of == 2:
        one = jax.random.randint(key, (), max(1, total - reach), min(reach, total - 1) + 1)
        return jnp.stack([one, total - one])
    sizes = jnp.asarray(profile(number_of, total, reach, slope), jnp.int32)
    pairs = (number_of - 1) // 2
    donor, sink = sizes[1:1 + 2 * pairs:2], sizes[2:2 + 2 * pairs:2]
    room = jnp.minimum(donor - 1, reach - sink)
    passed = jax.random.randint(jax.random.fold_in(key, 1), (pairs,), 0, 1 << 20) % (room + 1)
    sizes = sizes.at[1:1 + 2 * pairs:2].set(donor - passed).at[2:2 + 2 * pairs:2].set(sink + passed)
    return sizes[jax.random.permutation(jax.random.fold_in(key, 2), number_of)]


def bell_draw(own_key, dims, scale, limit, shards=(), held_as=jnp.bfloat16):
    level = block_levels(own_key, dims, shards, -0.22, 0.18) if shards else 1.0
    array = jax.random.normal(own_key, dims, jnp.float32) * scale * level
    return jnp.minimum(jnp.maximum(array, -limit), limit).astype(held_as)


def setup_inputs(seed: int = 0) -> dict:
    arg_keys = jax.random.split(jax.random.key(seed), 9)
    return {
        "train_act": draw_train_act(jax.random.fold_in(arg_keys[8], 71), 0),
        "train_grad": draw_train_grad(jax.random.fold_in(arg_keys[8], 71), 0),
        "query_act": bell_draw(arg_keys[2], (QROWS, D), 1.0, 6.0, ((1, 32),)),
        "query_grad": bell_draw(arg_keys[3], (QROWS, FF), 1.0, 6.0, ((1, 32),)),
        "query_of": draw_query_of(jax.random.fold_in(arg_keys[8], 71), 0),
        "counts": uneven_parts(arg_keys[5], N_DP, N_DP * TOK_DEV * 3 // 4, TOK_DEV, 0).astype(jnp.int32),
        "eig_act": draw_eig_act(jax.random.fold_in(arg_keys[8], 71), 0),
        "eig_grad": draw_eig_grad(jax.random.fold_in(arg_keys[8], 71), 0),
    }


damping = 0.1

def reference(train_act, train_grad, query_act, query_grad, query_of, counts, eig_act, eig_grad):
    train_ra = jnp.dot(train_act, eig_act, preferred_element_type=jnp.float32).astype(jnp.bfloat16)
    train_rg = jnp.dot(train_grad, eig_grad, preferred_element_type=jnp.float32).astype(jnp.bfloat16)
    query_ra = jnp.dot(query_act, eig_act, preferred_element_type=jnp.float32).astype(jnp.bfloat16)
    query_rg = jnp.dot(query_grad, eig_grad, preferred_element_type=jnp.float32).astype(jnp.bfloat16)
    positions = jnp.arange(TOKENS, dtype=jnp.int32)
    shard_of = positions // TOK_DEV
    allowed = counts[shard_of]
    valid = (positions % TOK_DEV < allowed).astype(jnp.float32)
    squares_act = (train_ra.astype(jnp.float32) ** 2 * valid[:, None]).astype(jnp.bfloat16)
    squares_grad = (train_rg.astype(jnp.float32) ** 2).astype(jnp.bfloat16)

    def shard_sum(running, shard_num):
        act_part = lax.dynamic_slice_in_dim(squares_act, shard_num * TOK_DEV, TOK_DEV, 0)
        grad_part = lax.dynamic_slice_in_dim(squares_grad, shard_num * TOK_DEV, TOK_DEV, 0)
        partial_value = lax.dot_general(act_part, grad_part, (((0,), (0,)), ((), ())), preferred_element_type=jnp.float32)
        rounded = lax.optimization_barrier(partial_value.astype(jnp.bfloat16))
        return (running + rounded.astype(jnp.float32), None)
    summed, _ = lax.scan(shard_sum, jnp.zeros((D, FF), jnp.float32), jnp.arange(N_DP, dtype=jnp.int32))
    corrections = summed / jnp.sum(counts).astype(jnp.float32) + damping
    grouped = jnp.argsort(query_of, stable=True).reshape(QUERIES, QTOK)
    factor = 1.0 / math.sqrt(D * FF * QTOK)

    def one_query(members):
        act_sel = query_ra[members].astype(jnp.float32)
        grad_sel = query_rg[members].astype(jnp.float32)
        products = jnp.dot(act_sel.T, grad_sel, precision=lax.Precision.HIGHEST)
        weighted = (products / corrections).astype(jnp.bfloat16)
        mixed_rows = jnp.dot(train_ra, weighted, preferred_element_type=jnp.float32)
        return lax.optimization_barrier(jnp.sum(mixed_rows * train_rg.astype(jnp.float32), axis=1)) * valid * factor
    scores = lax.map(one_query, grouped)
    return (scores, corrections)
```

```python
import functools
import math

import jax
import jax.numpy as jnp
from jax import lax
from jax.experimental import pallas as pl
from jax.experimental.pallas import tpu as pltpu
from jax.sharding import PartitionSpec as P

D = 4096
FF = 10240
QUERIES = 8
QTOK = 2
damping = 0.1

MESH = pl.DeviceIdType.MESH
BF = jnp.bfloat16
F32 = jnp.float32

TOK = 128
AC = 128
GC = 320
QR = 16
AR = TOK + QR


def mod(value, size):
    return lax.rem(value + size, size)


def device(x, l, k, h, z):
    return (x * 4 + l * 2 + k, h * 8 + z)


def kernel(ta, tg, qa, qg, qof, cnt, ea, eg, sc_out, corr_out,
           blk_a, act, ea2, ebuf, ss1, qmsg, qb, sbuf, sq, acc, pb, rsb, qpb, rgb, rg,
           rab, rs1, ra, raq, wts, fsc, f1, f2, f3, *sems):
    (a_s, a_r, ar_s, ar_r, e_s, e_r, s0_s, s0_r, s1_s, s1_r, s2_s, s2_r,
     sr_s, sr_r, sq_s, sq_r, rs_s, rs_r, rq_s, rq_r, ag_s, ag_r, fw_s, fw_r,
     r0_s, r0_r, r1_s, r1_r, r2_s, r2_r, rr_s, rr_r, rk_s, rk_r,
     f1_s, f1_r, f2_s, f2_r, f3_s, f3_r, loc) = sems
    dp, owner = lax.axis_index("dp"), lax.axis_index("owner")
    x, l, k = dp // 4, (dp // 2) % 2, dp % 2
    h, z = owner // 8, owner % 8
    za, zr = z // 4, z % 4
    swap = za != l
    partner = device(x, za, k, h, 4 * l + zr)
    chip = l * 4 + x
    shard = chip * 2 + k
    zp, zm = mod(z + 1, 8), mod(z - 1, 8)
    core = device(x, l, 1 - k, h, z)
    up, down = device(x, l, k, h, zp), device(x, l, k, h, zm)

    pending = []

    def copy(src, dst, ss, rs, to):
        return pltpu.make_async_remote_copy(
            src_ref=src, dst_ref=dst, send_sem=ss, recv_sem=rs, device_id=to, device_id_type=MESH)

    def send(src, dst, ss, rs, to, when=None):
        c = copy(src, dst, ss, rs, to)
        if when is None:
            c.start()
        else:
            pl.when(when)(lambda: c.start())
        pending.append((c, when))

    def arrived(dst, rs, when=None):
        c = copy(dst, dst, rs, rs, core)
        if when is None:
            c.wait_recv()
        else:
            pl.when(when)(lambda: c.wait_recv())

    bar = pltpu.get_barrier_semaphore()
    peers = [device(x, l, k, mod(h + j, 4), z) for j in range(1, 4)]
    peers += [device(x, l, k, h, mod(z + j, 8)) for j in range(1, 8)]

    def plane(s):
        return device((s // 2) % 4, s // 8, s % 2, h, z)

    peers += [plane(mod(shard + j, 16)) for j in range(1, 16)]
    for p in peers:
        pl.semaphore_signal(bar, inc=1, device_id=p, device_id_type=MESH)

    @pl.when(swap)
    def _():
        pl.semaphore_signal(bar, inc=1, device_id=partner, device_id_type=MESH)
    blk_a[0:TOK, :] = ta[...]
    blk_a[TOK:AR, :] = qa[...]
    qmsg[...] = jnp.zeros_like(qmsg)
    qmsg[:, 0:GC] = qg[...]

    @pl.when(swap)
    def _():
        pl.semaphore_wait(bar, len(peers) + 1)

    @pl.when(jnp.logical_not(swap))
    def _():
        pl.semaphore_wait(bar, len(peers))

    def act_slot(pos, lo=0, n=4):
        return act.at[:, pl.ds(pl.multiple_of(pos * 512 + lo * 128, 128), n * 128)]

    def act_one(pos, hh):
        return act.at[:, pl.ds(pl.multiple_of(pos * 512 + hh * 128, 128), 128)]

    for j in range(1, 4):
        send(blk_a, act_one(z, h), a_s.at[j], a_r.at[j], device(x, l, k, mod(h + j, 4), z))
    own_act = pltpu.make_async_copy(blk_a, act_one(z, h), loc.at[0])
    own_act.start()

    send(tg, ss1.at[h], s0_s.at[0], s0_r.at[0], partner, swap)
    send(qmsg, qb, s0_s.at[1], s0_r.at[1], partner, swap)
    send(eg, ebuf.at[k], e_s, e_r, core)

    @pl.when(jnp.logical_not(swap))
    def _():
        ss1[h] = tg[...]
        qb[...] = qmsg[...]
    ebuf[k] = eg[...]
    for zz in range(8):
        for hh in range(4):
            ea2[pl.ds(zz * 512 + hh * 128, 128), :] = ea[pl.ds(hh * 1024 + zz * 128, 128), :]

    own_act.wait()
    for j in range(1, 4):
        arrived(act_one(z, mod(h - j, 4)), a_r.at[j])

    def act_ring(hop):
        n = 4 if hop < 4 else 2
        pos = mod(z - hop + 1, 8)
        send(act_slot(pos, 0, n), act_slot(pos, 0, n), ar_s.at[0, hop - 1], ar_r.at[0, hop - 1], up)
        pos = mod(z + hop - 1, 8)
        lo = 4 - n
        send(act_slot(pos, lo, n), act_slot(pos, lo, n), ar_s.at[1, hop - 1], ar_r.at[1, hop - 1], down)

    def act_got(hop):
        n = 4 if hop < 4 else 2
        arrived(act_slot(mod(z - hop, 8), 0, n), ar_r.at[0, hop - 1])
        arrived(act_slot(mod(z + hop, 8), 4 - n, n), ar_r.at[1, hop - 1])

    def act_dot(pos):
        return jnp.dot(act[:, pl.ds(pl.multiple_of(pos * 512, 512), 512)],
                       ea2[pl.ds(pl.multiple_of(pos * 512, 512), 512), :],
                       preferred_element_type=F32)

    act_ring(1)
    arrived(ss1.at[h], s0_r.at[0], swap)
    arrived(qb, s0_r.at[1], swap)
    for j in range(1, 4):
        to = device(x, l, k, mod(h + j, 4), z)
        send(ss1.at[h], ss1.at[h], s1_s.at[j], s1_r.at[j], to)
        send(qb, sq.at[zr], s1_s.at[3 + j], s1_r.at[0], to, h == x)
    total = act_dot(z)
    act_got(1)
    act_ring(2)
    total += act_dot(mod(z - 1, 8)) + act_dot(mod(z + 1, 8))

    for j in range(1, 4):
        hh = mod(h - j, 4)
        arrived(ss1.at[hh], s1_r.at[j])

    def s_slot(pos, half=None, xx=None):
        if xx is not None:
            lanes = pl.ds(pl.multiple_of(xx * 128, 128), 128)
        else:
            lanes = pl.ds(half * 256, 256)
        return sbuf.at[pos // 4, pl.ds(pl.multiple_of((pos % 4) * GC, GC), GC), lanes]

    for j in range(1, 4):
        xt = mod(x + j, 4)
        send(ss1.at[xt], s_slot(z, xx=x), s2_s.at[j], s2_r.at[j], device(xt, l, k, h, z))
    own_s = pltpu.make_async_copy(ss1.at[x], s_slot(z, xx=x), loc.at[1])
    own_s.start()

    @pl.when(h == x)
    def _():
        sq[zr] = qb[...]
    arrived(sq.at[zr], s1_r.at[0], h != x)

    act_got(2)
    act_ring(3)
    total += act_dot(mod(z - 2, 8)) + act_dot(mod(z + 2, 8))

    own_s.wait()
    for j in range(1, 4):
        arrived(s_slot(z, xx=mod(x - j, 4)), s2_r.at[j])

    def s_ring(half, hop):
        if hop < 4 or half == 0:
            pos = mod(z - hop + 1, 8)
            send(s_slot(pos, half), s_slot(pos, half), sr_s.at[0, half, hop - 1], sr_r.at[0, half, hop - 1], up)
        if hop < 4 or half == 1:
            pos = mod(z + hop - 1, 8)
            send(s_slot(pos, half), s_slot(pos, half), sr_s.at[1, half, hop - 1], sr_r.at[1, half, hop - 1], down)

    def s_got(half, hop):
        if hop < 4 or half == 0:
            arrived(s_slot(mod(z - hop, 8), half), sr_r.at[0, half, hop - 1])
        if hop < 4 or half == 1:
            arrived(s_slot(mod(z + hop, 8), half), sr_r.at[1, half, hop - 1])

    s_ring(0, 1)
    s_ring(1, 1)
    send(sq.at[zr], sq.at[zr], sq_s.at[0], sq_r.at[0], up)
    send(sq.at[zr], sq.at[zr], sq_s.at[1], sq_r.at[1], down)

    act_got(3)
    act_ring(4)
    total += act_dot(mod(z - 3, 8)) + act_dot(mod(z + 3, 8))
    acc[...] = jnp.zeros_like(acc)
    arrived(ebuf.at[1 - k], e_r)
    act_got(4)
    total += act_dot(mod(z + 4, 8))
    rab[...] = total.astype(BF)

    send(rab, rs1.at[h], r0_s, r0_r, partner, swap)

    @pl.when(jnp.logical_not(swap))
    def _():
        rs1[h] = rab[...]

    pair = z // 2
    step = 2 * (z % 2) - 1
    order = [pair, mod(pair + step, 4), mod(pair - step, 4), mod(pair + 2, 4)]

    def s_dot(g, half):
        la, m = g // 2, g % 2
        acc[la, :, half * 256:half * 256 + 256] += jnp.dot(
            ebuf[m], sbuf[la, pl.ds(pl.multiple_of(m * 640, 640), 640), half * 256:half * 256 + 256],
            preferred_element_type=F32)

    s_got(0, 1)
    s_ring(0, 2)
    s_got(1, 1)
    s_ring(1, 2)
    arrived(sq.at[mod(zr - 1, 4)], sq_r.at[0])
    arrived(sq.at[mod(zr + 1, 4)], sq_r.at[1])
    send(sq.at[mod(zr - 1, 4)], sq.at[mod(zr - 1, 4)], sq_s.at[2], sq_r.at[2], up)
    s_dot(order[0], 0)
    s_dot(order[0], 1)

    arrived(rs1.at[h], r0_r, swap)
    for j in range(1, 4):
        send(rs1.at[h], rs1.at[h], r1_s.at[j], r1_r.at[j], device(x, l, k, mod(h + j, 4), z))

    s_got(0, 2)
    s_ring(0, 3)
    s_got(1, 2)
    s_ring(1, 3)
    s_dot(order[1], 0)
    s_dot(order[1], 1)

    for j in range(1, 4):
        arrived(rs1.at[mod(h - j, 4)], r1_r.at[j])
    kt = zr // 2
    mine = k == kt

    def ra_block(pos, xx, kk):
        return ra.at[pos // 4, pl.ds(pl.multiple_of(xx * 256 + kk * 128, 128), 128),
                     pl.ds(pl.multiple_of((pos % 2) * 128, 128), 128)]

    def ra_slot(pos, half):
        return ra.at[pos // 4, pl.ds(half * 512, 512), pl.ds(pl.multiple_of((pos % 2) * 128, 128), 128)]

    for j in range(1, 4):
        xt = mod(x + j, 4)
        send(rs1.at[xt, pl.ds(0, TOK), :], ra_block(z, x, k), r2_s.at[j], r2_r.at[j], device(xt, l, k, h, z), mine)
    for j in range(4):
        xt = mod(x + j, 4)
        send(rs1.at[xt, pl.ds(0, TOK), :], ra_block(z, x, k), r2_s.at[4 + j], r2_r.at[4 + j],
             device(xt, l, 1 - k, h, z), jnp.logical_not(mine))

    def raq_slot(pos):
        return raq.at[:, pl.ds(pl.multiple_of((pos % 2) * 128, 128), 128)]

    @pl.when(mine)
    def _():
        a = pltpu.make_async_copy(rs1.at[x, pl.ds(0, TOK), :], ra_block(z, x, k), loc.at[2])
        b = pltpu.make_async_copy(rs1.at[x, pl.ds(TOK, QR), :], raq_slot(z), loc.at[3])
        a.start()
        b.start()
        a.wait()
        b.wait()

    s_got(0, 3)
    s_ring(0, 4)
    s_got(1, 3)
    s_ring(1, 4)
    s_dot(order[2], 0)
    s_dot(order[2], 1)

    for j in range(1, 4):
        arrived(ra_block(z, mod(x - j, 4), k), r2_r.at[j], mine)
    for j in range(4):
        arrived(ra_block(z, mod(x - j, 4), 1 - k), r2_r.at[4 + j], mine)

    def held(pos):
        return (pos % 4) // 2 == k

    def r_ring(hop):
        for half in range(2):
            if hop < 4 or half == 0:
                pos = mod(z - hop + 1, 8)
                send(ra_slot(pos, half), ra_slot(pos, half), rr_s.at[0, half, hop - 1], rr_r.at[0, half, hop - 1],
                     up, held(pos))
            if hop < 4 or half == 1:
                pos = mod(z + hop - 1, 8)
                send(ra_slot(pos, half), ra_slot(pos, half), rr_s.at[1, half, hop - 1], rr_r.at[1, half, hop - 1],
                     down, held(pos))

    def r_got(hop):
        for half in range(2):
            if hop < 4 or half == 0:
                pos = mod(z - hop, 8)
                arrived(ra_slot(pos, half), rr_r.at[0, half, hop - 1], held(pos))
            if hop < 4 or half == 1:
                pos = mod(z + hop, 8)
                arrived(ra_slot(pos, half), rr_r.at[1, half, hop - 1], held(pos))

    r_ring(1)
    send(raq_slot(z), raq_slot(z), rk_s.at[0], rk_r.at[0], up, held(z))
    send(raq_slot(z), raq_slot(z), rk_s.at[1], rk_r.at[1], down, held(z))

    s_got(0, 4)
    s_got(1, 4)
    s_dot(order[3], 0)
    s_dot(order[3], 1)
    for b in range(8):
        pb[b] = acc[b // 4, :, (b % 4) * 128:(b % 4) * 128 + 128].astype(BF)
        send(pb.at[b], rsb.at[chip], rs_s.at[b], rs_r.at[chip], device(b % 4, b // 4, k, h, z), chip != b)

    arrived(sq.at[mod(zr - 2, 4)], sq_r.at[2])
    qpart = jnp.zeros((QR, GC), F32)
    for m in range(2):
        zero = jnp.zeros((QR, 384), F32)
        first = jnp.concatenate([sq[2 * m].astype(F32), zero], axis=1)
        second = jnp.concatenate([sq[2 * m + 1].astype(F32), zero], axis=1)
        both = (first + pltpu.roll(second, GC, 1))[:, 0:640].astype(BF)
        qpart += lax.dot_general(both, ebuf[m], (((1,), (1,)), ((), ())), preferred_element_type=F32)
    qpb[chip] = jnp.concatenate([qpart, jnp.zeros((QR, 64), F32)], axis=1)
    for b in range(8):
        send(qpb.at[chip], qpb.at[chip], rq_s.at[b], rq_r.at[chip], device(b % 4, b // 4, k, h, z), chip != b)

    r_got(1)
    r_ring(2)
    pos = mod(z - 1, 8)
    arrived(raq_slot(pos), rk_r.at[0], held(pos))
    send(raq_slot(pos), raq_slot(pos), rk_s.at[2], rk_r.at[2], up, held(pos))
    pos = mod(z + 1, 8)
    arrived(raq_slot(pos), rk_r.at[1], held(pos))

    rsb[chip] = pb[chip]
    for b in range(8):
        arrived(rsb.at[b], rs_r.at[b], chip != b)
    block = rsb[0].astype(F32)
    for b in range(1, 8):
        block += rsb[b].astype(F32)
    rgb[...] = block.astype(BF)

    def rg_slot(s):
        return rg.at[:, pl.ds(pl.multiple_of(s * 128, 128), 128)]

    for b in range(8):
        send(rgb, rg_slot(shard), ag_s.at[b], ag_r.at[chip], device(b % 4, b // 4, k, h, z), chip != b)
    send(rgb, rg_slot(shard), fw_s.at[chip], fw_r.at[chip], core)
    own_rg = pltpu.make_async_copy(rgb, rg_slot(shard), loc.at[4])
    own_rg.start()

    r_got(2)
    r_ring(3)
    for b in range(8):
        arrived(rg_slot(2 * b + k), ag_r.at[b], chip != b)
        send(rg_slot(2 * b + k), rg_slot(2 * b + k), fw_s.at[b], fw_r.at[b], core, chip != b)
    r_got(3)
    r_ring(4)
    pos = mod(z - 2, 8)
    arrived(raq_slot(pos), rk_r.at[2], held(pos))
    own_rg.wait()
    for b in range(8):
        arrived(rg_slot(2 * b + 1 - k), fw_r.at[b])
    r_got(4)

    tokens = 0
    for s in range(16):
        tokens = tokens + cnt[s]
    tokens = tokens.astype(F32)
    corr_out[...] = jnp.zeros_like(corr_out)
    row = lax.broadcasted_iota(jnp.int32, (256, 1), 0)

    for c in range(8):
        s = (c % 4) * 4 + (c // 4) * 2
        limit = jnp.where(row < 128, cnt[s], cnt[s + 1] + 128)
        ok = (row < limit).astype(F32)
        a = ra[c // 4, (c % 4) * 256:(c % 4) * 256 + 256, :].astype(F32)
        g = rg[:, c * 256:c * 256 + 256].astype(F32)
        corr_out[...] += jnp.dot((g * g).astype(BF), (a * a * ok).astype(BF), preferred_element_type=F32)
    corr = corr_out[...] / tokens + damping
    corr_out[...] = corr

    for b in range(8):
        arrived(qpb.at[b], rq_r.at[b], chip != b)
    qsum = qpb[0]
    for b in range(1, 8):
        qsum += qpb[b]
    qrows = qsum.astype(BF).astype(F32)
    lane = lax.broadcasted_iota(jnp.int32, (QR, 384), 0)
    of = jnp.zeros((QR, 384), jnp.int32)
    for s in range(QR):
        of = jnp.where(lane == s, qof[s], of)
    for q in range(QUERIES):
        picked = jnp.where(of == q, qrows, 0.0).T.astype(BF)[0:GC, :]
        prod = jnp.dot(picked, raq[...], preferred_element_type=F32)
        wts[q] = (prod / corr_out[...]).astype(BF)

    def chunk(c, carry):
        rac = ra[c // 4, pl.ds(pl.multiple_of((c % 4) * 256, 256), 256), :]
        rgc = rg[:, pl.ds(pl.multiple_of(c * 256, 256), 256)].astype(F32)
        rows = []
        for q in range(QUERIES):
            mixed = lax.dot_general(wts[q], rac, (((1,), (1,)), ((), ())), preferred_element_type=F32)
            rows.append(jnp.sum(mixed * rgc, axis=0, keepdims=True))
        fsc[:, pl.ds(pl.multiple_of(c * 256, 256), 256)] = jnp.concatenate(rows, axis=0)
        return carry

    lax.fori_loop(0, 8, chunk, 0)

    for s in range(16):
        send(fsc.at[:, pl.ds(s * 128, 128)], f1.at[shard], f1_s.at[s], f1_r.at[shard],
             device((s // 2) % 4, s // 8, s % 2, h, z), shard != s)
    f1[shard] = fsc[:, pl.ds(pl.multiple_of(shard * 128, 128), 128)]
    for s in range(16):
        arrived(f1.at[s], f1_r.at[s], shard != s)
    part = f1[0]
    for s in range(1, 16):
        part += f1[s]
    f2[h] = part
    for j in range(1, 4):
        send(f2.at[h], f2.at[h], f2_s.at[j], f2_r.at[j], device(x, l, k, mod(h + j, 4), z))
    for j in range(1, 4):
        arrived(f2.at[mod(h - j, 4)], f2_r.at[j])
    f3[z] = f2[0] + f2[1] + f2[2] + f2[3]
    for j in range(1, 8):
        send(f3.at[z], f3.at[z], f3_s.at[j], f3_r.at[j], device(x, l, k, h, mod(z + j, 8)))
    for j in range(1, 8):
        arrived(f3.at[mod(z - j, 8)], f3_r.at[j])
    done = f3[0]
    for j in range(1, 8):
        done += f3[j]
    t = lax.broadcasted_iota(jnp.int32, (8, 128), 1)
    done = jnp.where(t < cnt[dp], done, 0.0) * (1.0 / math.sqrt(D * FF * QTOK))
    sc_out[...] = pltpu.roll(done, mod(128 - 4 * owner, 128), 1)

    for c, when in pending:
        if when is None:
            c.wait_send()
        else:
            pl.when(when)(functools.partial(lambda c: c.wait_send(), c))


def per_device(train_act, train_grad, query_act, query_grad, query_of, counts, eig_act, eig_grad):
    vm = pl.BlockSpec(memory_space=pltpu.VMEM)
    sm = pl.BlockSpec(memory_space=pltpu.SMEM)
    V = pltpu.VMEM
    dma = pltpu.SemaphoreType.DMA
    scratch = [
        V((AR, AC), BF), V((AR, D), BF), V((D, AC), BF), V((2, GC, 640), BF),
        V((4, GC, TOK), BF), V((QR, 384), BF), V((QR, 384), BF), V((2, 1280, 512), BF), V((4, QR, 384), BF),
        V((2, GC, 512), F32), V((8, GC, TOK), BF), V((8, GC, TOK), BF), V((8, QR, 384), F32),
        V((GC, TOK), BF), V((GC, 2048), BF),
        V((AR, AC), BF), V((4, AR, AC), BF), V((2, 1024, 256), BF), V((QR, 256), BF),
        V((QUERIES, GC, 256), BF), V((8, 2048), F32), V((16, 8, 128), F32), V((4, 8, 128), F32), V((8, 8, 128), F32),
    ]
    counts_of = [
        (4,), (4,), (2, 4), (2, 4), (), (), (2,), (2,), (7,), (4,), (4,), (4,),
        (2, 2, 4), (2, 2, 4), (3,), (3,), (8,), (8,), (8,), (8,), (8,), (8,), (8,), (8,),
        (), (), (4,), (4,), (8,), (8,), (2, 2, 4), (2, 2, 4), (3,), (3,),
        (16,), (16,), (4,), (4,), (8,), (8,), (5,),
    ]
    scratch += [dma(n) if n else dma for n in counts_of]
    scores, corr = pl.pallas_call(
        kernel,
        out_shape=(jax.ShapeDtypeStruct((8, 128), F32), jax.ShapeDtypeStruct((GC, 256), F32)),
        in_specs=[vm, vm, vm, vm, sm, sm, vm, vm],
        out_specs=(vm, vm),
        scratch_shapes=scratch,
        compiler_params=pltpu.CompilerParams(
            collective_id=0, has_side_effects=True, vmem_limit_bytes=48 * 2**20),
    )(train_act, train_grad.T, query_act, query_grad, query_of, counts, eig_act, eig_grad.T)
    return scores[:, :4], corr.T


def solution(mesh):
    in_specs = (
        P("dp", "owner"),
        P("dp", "owner"),
        P(None, "owner"),
        P(None, "owner"),
        P(),
        P(),
        P(None, "owner"),
        P("dp", "owner"),
    )
    out_specs = (P(None, ("dp", "owner")), P("dp", "owner"))
    return jax.shard_map(
        per_device, mesh=mesh, in_specs=in_specs, out_specs=out_specs, check_vma=False
    )
```

```python
import functools
import math

import jax
import jax.numpy as jnp
from jax import lax
from jax.experimental import pallas as pl
from jax.experimental.pallas import tpu as pltpu
from jax.sharding import PartitionSpec as P

D = 4096
FF = 10240
QUERIES = 8
QTOK = 2
damping = 0.1

MESH = pl.DeviceIdType.MESH
BF = jnp.bfloat16
F32 = jnp.float32

TOK = 128
AC = 128
GC = 320
QR = 16
AR = TOK + QR


def mod(value, size):
    return lax.rem(value + size, size)


def device(x, l, k, h, z):
    return (x * 4 + l * 2 + k, h * 8 + z)


def kernel(ta, tg, qa, qg, qof_in, cnt_in, ea, eg, sc_out, corr_out,
           qof, cnt, qgv, tgv, ld, blk_a, act, ea2, ebuf, qmsg, gbuf, sq, acc, qpb, rgb, rg,
           rab, rs1, ra, raq, wts, fsc, f1, f2, f3, *sems):
    (a_s, a_r, ar_s, ar_r, ec_s, ec_r, ex_s, ex_r, s1_s, s1_r,
     sr_s, sr_r, sq_s, sq_r, rq_s, rq_r, ag_s, ag_r, fw_s, fw_r,
     r0_s, r0_r, r1_s, r1_r, r2_s, r2_r, rr_s, rr_r, rk_s, rk_r,
     f1_s, f1_r, f2_s, f2_r, f3_s, f3_r, loc) = sems
    dp, owner = lax.axis_index("dp"), lax.axis_index("owner")
    x, l, k = dp // 4, (dp // 2) % 2, dp % 2
    h, z = owner // 8, owner % 8
    za, zr = z // 4, z % 4
    swap = za != l
    partner = device(x, za, k, h, 4 * l + zr)
    chip = l * 4 + x
    shard = chip * 2 + k
    zp, zm = mod(z + 1, 8), mod(z - 1, 8)
    core = device(x, l, 1 - k, h, z)
    up, down = device(x, l, k, h, zp), device(x, l, k, h, zm)

    pending = []

    def copy(src, dst, ss, rs, to):
        return pltpu.make_async_remote_copy(
            src_ref=src, dst_ref=dst, send_sem=ss, recv_sem=rs, device_id=to, device_id_type=MESH)

    def send(src, dst, ss, rs, to, when=None):
        c = copy(src, dst, ss, rs, to)
        if when is None:
            c.start()
        else:
            pl.when(when)(lambda: c.start())
        pending.append((c, when))

    def arrived(dst, rs, when=None):
        c = copy(dst, dst, rs, rs, core)
        if when is None:
            c.wait_recv()
        else:
            pl.when(when)(lambda: c.wait_recv())

    bar = pltpu.get_barrier_semaphore()
    peers = [device(x, l, k, mod(h + j, 4), z) for j in range(1, 4)]
    peers += [device(x, l, k, h, mod(z + j, 8)) for j in range(1, 8)]

    def plane(s):
        return device((s // 2) % 4, s // 8, s % 2, h, z)

    peers += [plane(mod(shard + j, 16)) for j in range(1, 16)]
    for p in peers:
        pl.semaphore_signal(bar, inc=1, device_id=p, device_id_type=MESH)

    @pl.when(swap)
    def _():
        pl.semaphore_signal(bar, inc=1, device_id=partner, device_id_type=MESH)

    def local(src, dst, sem):
        c = pltpu.make_async_copy(src, dst, sem)
        c.start()
        return c

    loads = [local(ta, blk_a.at[pl.ds(0, TOK), :], ld.at[0]), local(qa, blk_a.at[pl.ds(TOK, QR), :], ld.at[1]),
             local(qg, qgv, ld.at[2]), local(tg, tgv, ld.at[3]), local(eg, ebuf.at[dp], ld.at[4]),
             local(qof_in, qof, ld.at[5]), local(cnt_in, cnt, ld.at[6])]
    loads += [local(ea.at[hh], ea2.at[:, hh], ld.at[7 + hh]) for hh in range(4)]
    for c in loads:
        c.wait()
    qmsg[...] = jnp.zeros_like(qmsg)
    qmsg[:, 0:GC] = qgv[...]

    @pl.when(swap)
    def _():
        pl.semaphore_wait(bar, len(peers) + 1)

    @pl.when(jnp.logical_not(swap))
    def _():
        pl.semaphore_wait(bar, len(peers))

    def act_slot(pos, lo=0, n=4):
        return act.at[:, pl.ds(pl.multiple_of(pos * 512 + lo * 128, 128), n * 128)]

    def act_one(pos, hh):
        return act.at[:, pl.ds(pl.multiple_of(pos * 512 + hh * 128, 128), 128)]

    for j in range(1, 4):
        send(blk_a, act_one(z, h), a_s.at[j], a_r.at[j], device(x, l, k, mod(h + j, 4), z))
    own_act = local(blk_a, act_one(z, h), loc.at[0])

    def g_one(pos, hh):
        return gbuf.at[hh, pl.ds(pl.multiple_of(pos * GC, GC), GC), :]

    def g_slot(pos, half):
        return gbuf.at[pl.ds(half * 2, 2), pl.ds(pl.multiple_of(pos * GC, GC), GC), :]

    for j in range(1, 4):
        send(tgv, g_one(z, h), s1_s.at[j], s1_r.at[j], device(x, l, k, mod(h + j, 4), z))
    own_g = local(tgv, g_one(z, h), loc.at[1])

    for j in range(1, 4):
        send(qmsg, sq.at[zr], sq_s.at[j], sq_r.at[7], device(x, l, k, mod(h + j, 4), z),
             jnp.logical_and(h == x, za == l))

    @pl.when(jnp.logical_and(h == x, za == l))
    def _():
        sq[zr] = qmsg[...]

    def e_at(xx, ll, part=None):
        d = xx * 4 + ll * 2 + k
        if part is None:
            return ebuf.at[d]
        return ebuf.at[d, pl.ds(part * 160, 160), :]

    xp, xm, xo = mod(x + 1, 4), mod(x - 1, 4), mod(x + 2, 4)
    right, left = device(xp, l, k, h, z), device(xm, l, k, h, z)
    beside = device(x, 1 - l, k, h, z)

    def e_pass(xx, ll, i):
        send(e_at(xx, ll), e_at(xx, ll), ec_s.at[i], ec_r.at[i], core)

    send(e_at(x, l), e_at(x, l), ex_s.at[0], ex_r.at[0], beside)
    send(e_at(x, l), e_at(x, l), ex_s.at[1], ex_r.at[1], right)
    send(e_at(x, l), e_at(x, l), ex_s.at[2], ex_r.at[2], left)
    e_pass(x, l, 0)

    own_act.wait()
    for j in range(1, 4):
        arrived(act_one(z, mod(h - j, 4)), a_r.at[j])

    def act_ring(hop):
        n = 4 if hop < 4 else 2
        pos = mod(z - hop + 1, 8)
        send(act_slot(pos, 0, n), act_slot(pos, 0, n), ar_s.at[0, hop - 1], ar_r.at[0, hop - 1], up)
        pos = mod(z + hop - 1, 8)
        lo = 4 - n
        send(act_slot(pos, lo, n), act_slot(pos, lo, n), ar_s.at[1, hop - 1], ar_r.at[1, hop - 1], down)

    def act_got(hop):
        n = 4 if hop < 4 else 2
        arrived(act_slot(mod(z - hop, 8), 0, n), ar_r.at[0, hop - 1])
        arrived(act_slot(mod(z + hop, 8), 4 - n, n), ar_r.at[1, hop - 1])

    def act_dot(pos):
        return jnp.dot(act[:, pl.ds(pl.multiple_of(pos * 512, 512), 512)],
                       ea2[pos].reshape(512, 128),
                       preferred_element_type=F32)

    def s_ring(half, hop):
        if hop < 4 or half == 0:
            pos = mod(z - hop + 1, 8)
            send(g_slot(pos, half), g_slot(pos, half), sr_s.at[0, half, hop - 1], sr_r.at[0, half, hop - 1], up)
        if hop < 4 or half == 1:
            pos = mod(z + hop - 1, 8)
            send(g_slot(pos, half), g_slot(pos, half), sr_s.at[1, half, hop - 1], sr_r.at[1, half, hop - 1], down)

    def s_got(half, hop):
        if hop < 4 or half == 0:
            arrived(g_slot(mod(z - hop, 8), half), sr_r.at[0, half, hop - 1])
        if hop < 4 or half == 1:
            arrived(g_slot(mod(z + hop, 8), half), sr_r.at[1, half, hop - 1])

    act_ring(1)
    total = act_dot(z)
    own_g.wait()
    for j in range(1, 4):
        arrived(g_one(z, mod(h - j, 4)), s1_r.at[j])
    s_ring(0, 1)
    s_ring(1, 1)
    arrived(sq.at[zr], sq_r.at[7], jnp.logical_and(h != x, za == l))
    for j in range(1, 8):
        send(sq.at[zr], sq.at[zr], sq_s.at[3 + j], sq_r.at[j - 1],
             device(x, l, k, h, mod(z + j, 8)), za == l)
    act_got(1)
    act_ring(2)
    total += act_dot(mod(z - 1, 8)) + act_dot(mod(z + 1, 8))

    arrived(e_at(x, 1 - l), ex_r.at[0])
    send(e_at(x, 1 - l), e_at(x, 1 - l), ex_s.at[3], ex_r.at[3], right)
    send(e_at(x, 1 - l), e_at(x, 1 - l), ex_s.at[4], ex_r.at[4], left)
    e_pass(x, 1 - l, 1)
    act_got(2)
    act_ring(3)
    total += act_dot(mod(z - 2, 8)) + act_dot(mod(z + 2, 8))

    arrived(e_at(xm, l), ex_r.at[1])
    send(e_at(xm, l, 0), e_at(xm, l, 0), ex_s.at[5], ex_r.at[5], right)
    e_pass(xm, l, 2)
    arrived(e_at(xp, l), ex_r.at[2])
    send(e_at(xp, l, 1), e_at(xp, l, 1), ex_s.at[6], ex_r.at[6], left)
    e_pass(xp, l, 3)

    act_got(3)
    act_ring(4)
    total += act_dot(mod(z - 3, 8)) + act_dot(mod(z + 3, 8))
    s_got(0, 1)
    s_ring(0, 2)
    s_got(1, 1)
    s_ring(1, 2)
    act_got(4)
    total += act_dot(mod(z + 4, 8))
    rab[...] = total.astype(BF)

    send(rab, rs1.at[h], r0_s, r0_r, partner, swap)

    @pl.when(jnp.logical_not(swap))
    def _():
        rs1[h] = rab[...]

    arrived(e_at(xm, 1 - l), ex_r.at[3])
    send(e_at(xm, 1 - l, 0), e_at(xm, 1 - l, 0), ex_s.at[7], ex_r.at[7], right)
    e_pass(xm, 1 - l, 4)
    arrived(e_at(xp, 1 - l), ex_r.at[4])
    send(e_at(xp, 1 - l, 1), e_at(xp, 1 - l, 1), ex_s.at[8], ex_r.at[8], left)
    e_pass(xp, 1 - l, 5)

    arrived(rs1.at[h], r0_r, swap)
    for j in range(1, 4):
        send(rs1.at[h], rs1.at[h], r1_s.at[j], r1_r.at[j], device(x, l, k, mod(h + j, 4), z))

    s_got(0, 2)
    s_ring(0, 3)
    s_got(1, 2)
    s_ring(1, 3)

    for j in range(1, 4):
        arrived(rs1.at[mod(h - j, 4)], r1_r.at[j])
    kt = zr // 2
    mine = k == kt

    def ra_block(pos, xx, kk):
        return ra.at[pos // 4, pl.ds(pl.multiple_of(xx * 256 + kk * 128, 128), 128),
                     pl.ds(pl.multiple_of((pos % 2) * 128, 128), 128)]

    def ra_slot(pos, half):
        return ra.at[pos // 4, pl.ds(half * 512, 512), pl.ds(pl.multiple_of((pos % 2) * 128, 128), 128)]

    for j in range(1, 4):
        xt = mod(x + j, 4)
        send(rs1.at[xt, pl.ds(0, TOK), :], ra_block(z, x, k), r2_s.at[j], r2_r.at[j], device(xt, l, k, h, z), mine)
    for j in range(4):
        xt = mod(x + j, 4)
        send(rs1.at[xt, pl.ds(0, TOK), :], ra_block(z, x, k), r2_s.at[4 + j], r2_r.at[4 + j],
             device(xt, l, 1 - k, h, z), jnp.logical_not(mine))

    def raq_slot(pos):
        return raq.at[:, pl.ds(pl.multiple_of((pos % 2) * 128, 128), 128)]

    @pl.when(mine)
    def _():
        a = pltpu.make_async_copy(rs1.at[x, pl.ds(0, TOK), :], ra_block(z, x, k), loc.at[2])
        b = pltpu.make_async_copy(rs1.at[x, pl.ds(TOK, QR), :], raq_slot(z), loc.at[3])
        a.start()
        b.start()
        a.wait()
        b.wait()

    arrived(e_at(xo, l, 0), ex_r.at[5])
    arrived(e_at(xo, l, 1), ex_r.at[6])
    e_pass(xo, l, 6)
    arrived(e_at(xo, 1 - l, 0), ex_r.at[7])
    arrived(e_at(xo, 1 - l, 1), ex_r.at[8])
    e_pass(xo, 1 - l, 7)

    s_got(0, 3)
    s_ring(0, 4)
    s_got(1, 3)
    s_ring(1, 4)

    for j in range(1, 4):
        arrived(ra_block(z, mod(x - j, 4), k), r2_r.at[j], mine)
    for j in range(4):
        arrived(ra_block(z, mod(x - j, 4), 1 - k), r2_r.at[4 + j], mine)

    def held(pos):
        return (pos % 4) // 2 == k

    def r_ring(hop):
        for half in range(2):
            if hop < 4 or half == 0:
                pos = mod(z - hop + 1, 8)
                send(ra_slot(pos, half), ra_slot(pos, half), rr_s.at[0, half, hop - 1], rr_r.at[0, half, hop - 1],
                     up, held(pos))
            if hop < 4 or half == 1:
                pos = mod(z + hop - 1, 8)
                send(ra_slot(pos, half), ra_slot(pos, half), rr_s.at[1, half, hop - 1], rr_r.at[1, half, hop - 1],
                     down, held(pos))

    def r_got(hop):
        for half in range(2):
            if hop < 4 or half == 0:
                pos = mod(z - hop, 8)
                arrived(ra_slot(pos, half), rr_r.at[0, half, hop - 1], held(pos))
            if hop < 4 or half == 1:
                pos = mod(z + hop, 8)
                arrived(ra_slot(pos, half), rr_r.at[1, half, hop - 1], held(pos))

    r_ring(1)
    send(raq_slot(z), raq_slot(z), rk_s.at[0], rk_r.at[0], up, held(z))
    send(raq_slot(z), raq_slot(z), rk_s.at[1], rk_r.at[1], down, held(z))

    e_of = [(x, l), (x, 1 - l), (xm, l), (xp, l), (xm, 1 - l), (xp, 1 - l), (xo, l), (xo, 1 - l)]
    for i, (xx, ll) in enumerate(e_of):
        arrived(ebuf.at[xx * 4 + ll * 2 + 1 - k], ec_r.at[i])
    pair = z // 2
    step = 2 * (z % 2) - 1
    order = [pair, mod(pair + step, 4), mod(pair - step, 4), mod(pair + 2, 4)]

    def s_dot(n):
        out = jnp.zeros((GC, TOK), F32)
        for hh in range(4):
            out += jnp.dot(ebuf[hh * 4 + n], gbuf[hh, pl.ds(pl.multiple_of(n * 640, 640), 640), :],
                           preferred_element_type=F32)
        return out

    acc[...] = s_dot(order[0]) + s_dot(order[1])
    acc[...] += s_dot(order[2])

    for j in range(1, 8):
        from_z = mod(z - j, 8)
        arrived(sq.at[from_z % 4], sq_r.at[j - 1], from_z // 4 == l)
    qpart = jnp.zeros((QR, GC), F32)
    for m in range(2):
        zero = jnp.zeros((QR, 384), F32)
        first = jnp.concatenate([sq[2 * m].astype(F32), zero], axis=1)
        second = jnp.concatenate([sq[2 * m + 1].astype(F32), zero], axis=1)
        both = (first + pltpu.roll(second, GC, 1))[:, 0:640].astype(BF)
        qpart += lax.dot_general(both, ebuf[(x * 4 + l * 2) + m], (((1,), (1,)), ((), ())),
                                 preferred_element_type=F32)
    qpb[chip] = jnp.concatenate([qpart, jnp.zeros((QR, 64), F32)], axis=1)
    for b in range(8):
        send(qpb.at[chip], qpb.at[chip], rq_s.at[b], rq_r.at[chip], device(b % 4, b // 4, k, h, z), chip != b)

    s_got(0, 4)
    s_got(1, 4)
    rgb[...] = (acc[...] + s_dot(order[3])).astype(BF)

    def rg_slot(s):
        return rg.at[:, pl.ds(pl.multiple_of(s * 128, 128), 128)]

    for b in range(8):
        send(rgb, rg_slot(shard), ag_s.at[b], ag_r.at[chip], device(b % 4, b // 4, k, h, z), chip != b)
    send(rgb, rg_slot(shard), fw_s.at[chip], fw_r.at[chip], core)
    own_rg = local(rgb, rg_slot(shard), loc.at[4])

    r_got(1)
    r_ring(2)
    pos = mod(z - 1, 8)
    arrived(raq_slot(pos), rk_r.at[0], held(pos))
    send(raq_slot(pos), raq_slot(pos), rk_s.at[2], rk_r.at[2], up, held(pos))
    pos = mod(z + 1, 8)
    arrived(raq_slot(pos), rk_r.at[1], held(pos))

    r_got(2)
    r_ring(3)
    for b in range(8):
        arrived(rg_slot(2 * b + k), ag_r.at[b], chip != b)
        send(rg_slot(2 * b + k), rg_slot(2 * b + k), fw_s.at[b], fw_r.at[b], core, chip != b)
    r_got(3)
    r_ring(4)
    pos = mod(z - 2, 8)
    arrived(raq_slot(pos), rk_r.at[2], held(pos))
    own_rg.wait()
    for b in range(8):
        arrived(rg_slot(2 * b + 1 - k), fw_r.at[b])
    r_got(4)

    tokens = 0
    for s in range(16):
        tokens = tokens + cnt[s]
    tokens = tokens.astype(F32)
    corr_out[...] = jnp.zeros_like(corr_out)
    row = lax.broadcasted_iota(jnp.int32, (256, 1), 0)

    for c in range(8):
        s = (c % 4) * 4 + (c // 4) * 2
        limit = jnp.where(row < 128, cnt[s], cnt[s + 1] + 128)
        ok = (row < limit).astype(F32)
        a = ra[c // 4, (c % 4) * 256:(c % 4) * 256 + 256, :].astype(F32)
        g = rg[:, c * 256:c * 256 + 256].astype(F32)
        corr_out[...] += jnp.dot((g * g).astype(BF), (a * a * ok).astype(BF), preferred_element_type=F32)
    corr = corr_out[...] / tokens + damping
    corr_out[...] = corr

    for b in range(8):
        arrived(qpb.at[b], rq_r.at[b], chip != b)
    qsum = qpb[0]
    for b in range(1, 8):
        qsum += qpb[b]
    qrows = qsum.astype(BF).astype(F32)
    lane = lax.broadcasted_iota(jnp.int32, (QR, 384), 0)
    of = jnp.zeros((QR, 384), jnp.int32)
    for s in range(QR):
        of = jnp.where(lane == s, qof[s], of)
    for q in range(QUERIES):
        picked = jnp.where(of == q, qrows, 0.0).T.astype(BF)[0:GC, :]
        prod = jnp.dot(picked, raq[...], preferred_element_type=F32)
        wts[q] = (prod / corr_out[...]).astype(BF)

    def chunk(c, carry):
        rac = ra[c // 4, pl.ds(pl.multiple_of((c % 4) * 256, 256), 256), :]
        rgc = rg[:, pl.ds(pl.multiple_of(c * 256, 256), 256)].astype(F32)
        rows = []
        for q in range(QUERIES):
            mixed = lax.dot_general(wts[q], rac, (((1,), (1,)), ((), ())), preferred_element_type=F32)
            rows.append(jnp.sum(mixed * rgc, axis=0, keepdims=True))
        fsc[:, pl.ds(pl.multiple_of(c * 256, 256), 256)] = jnp.concatenate(rows, axis=0)
        return carry

    lax.fori_loop(0, 8, chunk, 0)

    for s in range(16):
        send(fsc.at[:, pl.ds(s * 128, 128)], f1.at[shard], f1_s.at[s], f1_r.at[shard],
             device((s // 2) % 4, s // 8, s % 2, h, z), shard != s)
    f1[shard] = fsc[:, pl.ds(pl.multiple_of(shard * 128, 128), 128)]
    for s in range(16):
        arrived(f1.at[s], f1_r.at[s], shard != s)
    part = f1[0]
    for s in range(1, 16):
        part += f1[s]
    f2[h] = part
    for j in range(1, 4):
        send(f2.at[h], f2.at[h], f2_s.at[j], f2_r.at[j], device(x, l, k, mod(h + j, 4), z))
    for j in range(1, 4):
        arrived(f2.at[mod(h - j, 4)], f2_r.at[j])
    f3[z] = f2[0] + f2[1] + f2[2] + f2[3]
    for j in range(1, 8):
        send(f3.at[z], f3.at[z], f3_s.at[j], f3_r.at[j], device(x, l, k, h, mod(z + j, 8)))
    for j in range(1, 8):
        arrived(f3.at[mod(z - j, 8)], f3_r.at[j])
    done = f3[0]
    for j in range(1, 8):
        done += f3[j]
    t = lax.broadcasted_iota(jnp.int32, (8, 128), 1)
    done = jnp.where(t < cnt[dp], done, 0.0) * (1.0 / math.sqrt(D * FF * QTOK))
    sc_out[...] = pltpu.roll(done, mod(128 - 4 * owner, 128), 1)

    for c, when in pending:
        if when is None:
            c.wait_send()
        else:
            pl.when(when)(functools.partial(lambda c: c.wait_send(), c))


def per_device(train_act, train_grad, query_act, query_grad, query_of, counts, eig_act, eig_grad):
    vm = pl.BlockSpec(memory_space=pltpu.VMEM)
    hb = pl.BlockSpec(memory_space=pltpu.HBM)
    V = pltpu.VMEM
    dma = pltpu.SemaphoreType.DMA
    scratch = [
        pltpu.SMEM((QR,), jnp.int32), pltpu.SMEM((16,), jnp.int32), V((QR, GC), BF), V((GC, TOK), BF), dma((11,)),
        V((AR, AC), BF), V((AR, D), BF), V((8, 4, AC, AC), BF), V((16, GC, 640), BF),
        V((QR, 384), BF), V((4, 8 * GC, TOK), BF), V((4, QR, 384), BF),
        V((GC, TOK), F32), V((8, QR, 384), F32), V((GC, TOK), BF), V((GC, 2048), BF),
        V((AR, AC), BF), V((4, AR, AC), BF), V((2, 1024, 256), BF), V((QR, 256), BF),
        V((QUERIES, GC, 256), BF), V((8, 2048), F32), V((16, 8, 128), F32), V((4, 8, 128), F32), V((8, 8, 128), F32),
    ]
    counts_of = [
        (4,), (4,), (2, 4), (2, 4), (8,), (8,), (9,), (9,), (4,), (4,),
        (2, 2, 4), (2, 2, 4), (11,), (8,), (8,), (8,), (8,), (8,), (8,), (8,),
        (), (), (4,), (4,), (8,), (8,), (2, 2, 4), (2, 2, 4), (3,), (3,),
        (16,), (16,), (4,), (4,), (8,), (8,), (5,),
    ]
    scratch += [dma(n) if n else dma for n in counts_of]
    scores, corr = pl.pallas_call(
        kernel,
        out_shape=(jax.ShapeDtypeStruct((8, 128), F32), jax.ShapeDtypeStruct((GC, 256), F32)),
        in_specs=[hb] * 8,
        out_specs=(vm, vm),
        scratch_shapes=scratch,
        compiler_params=pltpu.CompilerParams(
            collective_id=0, has_side_effects=True, vmem_limit_bytes=48 * 2**20),
    )(train_act, train_grad.T, query_act, query_grad, query_of, counts, eig_act.reshape(4, 8, AC, AC), eig_grad.T)
    return scores[:, :4], corr.T


def solution(mesh):
    in_specs = (
        P("dp", "owner"),
        P("dp", "owner"),
        P(None, "owner"),
        P(None, "owner"),
        P(),
        P(),
        P(None, "owner"),
        P("dp", "owner"),
    )
    out_specs = (P(None, ("dp", "owner")), P("dp", "owner"))
    return jax.shard_map(
        per_device, mesh=mesh, in_specs=in_specs, out_specs=out_specs, check_vma=False
    )
```

```python
import functools
import math

import jax
import jax.numpy as jnp
from jax import lax
from jax.experimental import pallas as pl
from jax.experimental.pallas import tpu as pltpu
from jax.sharding import PartitionSpec as P

D = 4096
FF = 10240
QUERIES = 8
QTOK = 2
damping = 0.1

MESH = pl.DeviceIdType.MESH
BF = jnp.bfloat16
F32 = jnp.float32

TOK = 128
AC = 128
GC = 320
QR = 16
AR = TOK + QR
AY = 80
GY = 240


def mod(value, size):
    return lax.rem(value + size, size)


def device(x, l, k, h, z):
    return (x * 4 + l * 2 + k, h * 8 + z)


def kernel(ta, tg, qa, qg, qof_in, cnt_in, ea, eg, sc_out, corr_out,
           qof, cnt, qgv, ld, act, ea2, ebuf, qmsg, gbuf, sq, acc, qpb, rgb, rg,
           rab, rs1, ra, raq, wts, fsc, f1, f2, f3, *sems):
    (a_s, a_r, ar_s, ar_r, ec_s, ec_r, ex_s, ex_r, s1_s, s1_r,
     az_s, az_r, gz_s, gz_r, c_s, c_r, gc_s, gc_r,
     sr_s, sr_r, sq_s, sq_r, rq_s, rq_r, ag_s, ag_r, fw_s, fw_r,
     r0_s, r0_r, r1_s, r1_r, r2_s, r2_r, rr_s, rr_r, rk_s, rk_r,
     f1_s, f1_r, f2_s, f2_r, f3_s, f3_r, loc) = sems
    dp, owner = lax.axis_index("dp"), lax.axis_index("owner")
    x, l, k = dp // 4, (dp // 2) % 2, dp % 2
    h, z = owner // 8, owner % 8
    za, zr = z // 4, z % 4
    swap = za != l
    partner = device(x, za, k, h, 4 * l + zr)
    chip = l * 4 + x
    shard = chip * 2 + k
    zp, zm = mod(z + 1, 8), mod(z - 1, 8)
    core = device(x, l, 1 - k, h, z)
    up, down = device(x, l, k, h, zp), device(x, l, k, h, zm)

    pending = []

    def copy(src, dst, ss, rs, to):
        return pltpu.make_async_remote_copy(
            src_ref=src, dst_ref=dst, send_sem=ss, recv_sem=rs, device_id=to, device_id_type=MESH)

    def send(src, dst, ss, rs, to, when=None):
        c = copy(src, dst, ss, rs, to)
        if when is None:
            c.start()
        else:
            pl.when(when)(lambda: c.start())
        pending.append((c, when))

    def arrived(dst, rs, when=None):
        c = copy(dst, dst, rs, rs, core)
        if when is None:
            c.wait_recv()
        else:
            pl.when(when)(lambda: c.wait_recv())

    bar = pltpu.get_barrier_semaphore()
    peers = [device(x, l, k, mod(h + j, 4), z) for j in range(1, 4)]
    peers += [device(x, l, k, h, mod(z + j, 8)) for j in range(1, 8)]

    def plane(s):
        return device((s // 2) % 4, s // 8, s % 2, h, z)

    peers += [plane(mod(shard + j, 16)) for j in range(1, 16)]
    for p in peers:
        pl.semaphore_signal(bar, inc=1, device_id=p, device_id_type=MESH)

    @pl.when(swap)
    def _():
        pl.semaphore_signal(bar, inc=1, device_id=partner, device_id_type=MESH)

    def local(src, dst, sem):
        c = pltpu.make_async_copy(src, dst, sem)
        c.start()
        return c

    loads = [local(ta, act.at[h, z, pl.ds(0, TOK), :], ld.at[0]),
             local(qa, act.at[h, z, pl.ds(TOK, QR), :], ld.at[1]),
             local(qg, qgv, ld.at[2]), local(tg, gbuf.at[h, z], ld.at[3]), local(eg, ebuf.at[dp], ld.at[4]),
             local(qof_in, qof, ld.at[5]), local(cnt_in, cnt, ld.at[6])]
    loads += [local(ea.at[hh], ea2.at[:, hh], ld.at[7 + hh]) for hh in range(4)]
    for c in loads:
        c.wait()
    qmsg[...] = jnp.zeros_like(qmsg)
    qmsg[:, 0:GC] = qgv[...]

    @pl.when(swap)
    def _():
        pl.semaphore_wait(bar, len(peers) + 1)

    @pl.when(jnp.logical_not(swap))
    def _():
        pl.semaphore_wait(bar, len(peers))

    hp, hm, ho = mod(h + 1, 4), mod(h - 1, 4), mod(h + 2, 4)
    above, below = device(x, l, k, hp, z), device(x, l, k, hm, z)

    def y_out(get, ss, rs):
        send(get(h, None), get(h, None), ss.at[0], rs.at[0], above)
        send(get(h, None), get(h, None), ss.at[1], rs.at[1], below)

    def y_mid(get, ss, rs):
        arrived(get(hm, None), rs.at[0])
        send(get(hm, 0), get(hm, 0), ss.at[2], rs.at[2], above)
        arrived(get(hp, None), rs.at[1])
        send(get(hp, 1), get(hp, 1), ss.at[3], rs.at[3], below)

    def y_in(get, rs):
        arrived(get(ho, 0), rs.at[2])
        arrived(get(ho, 1), rs.at[3])

    def act_y(hh, part):
        lo, n = ((0, AY), (0, 48), (48, AY - 48))[0 if part is None else part + 1]
        return act.at[hh, z, pl.ds(lo, n), :]

    def g_y(hh, part):
        lo, n = ((0, GY), (0, 128), (128, GY - 128))[0 if part is None else part + 1]
        return gbuf.at[hh, z, pl.ds(lo, n), :]

    def act_col(hh, part):
        zs = pl.ds(0, 8) if part is None else pl.ds(4 * part, 4)
        return act.at[hh, zs, pl.ds(AY, AR - AY), :]

    def g_col(hh, part):
        zs = pl.ds(0, 8) if part is None else pl.ds(4 * part, 4)
        return gbuf.at[hh, zs, pl.ds(GY, GC - GY), :]

    def act_z(pos):
        return act.at[h, pos, pl.ds(AY, AR - AY), :]

    def g_z(pos):
        return gbuf.at[h, pos, pl.ds(GY, GC - GY), :]

    y_out(act_y, a_s, a_r)
    y_out(g_y, s1_s, s1_r)
    for j in (1, 7, 2, 6, 3, 5, 4):
        send(act_z(z), act_z(z), az_s.at[j], az_r.at[j], device(x, l, k, h, mod(z + j, 8)))
    for j in (1, 7, 2, 6, 3, 5, 4):
        send(g_z(z), g_z(z), gz_s.at[j], gz_r.at[j], device(x, l, k, h, mod(z + j, 8)))

    for j in range(1, 4):
        send(qmsg, sq.at[zr], sq_s.at[j], sq_r.at[7], device(x, l, k, mod(h + j, 4), z),
             jnp.logical_and(h == x, za == l))

    @pl.when(jnp.logical_and(h == x, za == l))
    def _():
        sq[zr] = qmsg[...]

    def e_at(xx, ll, part=None):
        d = xx * 4 + ll * 2 + k
        if part is None:
            return ebuf.at[d]
        return ebuf.at[d, pl.ds(part * 160, 160), :]

    xp, xm, xo = mod(x + 1, 4), mod(x - 1, 4), mod(x + 2, 4)
    right, left = device(xp, l, k, h, z), device(xm, l, k, h, z)
    beside = device(x, 1 - l, k, h, z)

    def e_pass(xx, ll, i):
        send(e_at(xx, ll), e_at(xx, ll), ec_s.at[i], ec_r.at[i], core)

    send(e_at(x, l), e_at(x, l), ex_s.at[0], ex_r.at[0], beside)
    send(e_at(x, l), e_at(x, l), ex_s.at[1], ex_r.at[1], right)
    send(e_at(x, l), e_at(x, l), ex_s.at[2], ex_r.at[2], left)
    e_pass(x, l, 0)

    def act_slot(pos, lo=0, n=4):
        return act.at[pl.ds(lo, n), pos, pl.ds(0, AY), :]

    def g_slot(pos, half):
        return gbuf.at[pl.ds(half * 2, 2), pos, pl.ds(0, GY), :]

    def act_ring(hop):
        n = 4 if hop < 4 else 2
        pos = mod(z - hop + 1, 8)
        send(act_slot(pos, 0, n), act_slot(pos, 0, n), ar_s.at[0, hop - 1], ar_r.at[0, hop - 1], up)
        pos = mod(z + hop - 1, 8)
        lo = 4 - n
        send(act_slot(pos, lo, n), act_slot(pos, lo, n), ar_s.at[1, hop - 1], ar_r.at[1, hop - 1], down)

    def act_got(hop):
        n = 4 if hop < 4 else 2
        arrived(act_slot(mod(z - hop, 8), 0, n), ar_r.at[0, hop - 1])
        arrived(act_slot(mod(z + hop, 8), 4 - n, n), ar_r.at[1, hop - 1])

    def act_dot(pos):
        lhs = jnp.concatenate([act[hh, pos, 0:AY, :] for hh in range(4)], axis=1)
        return jnp.dot(lhs, ea2[pos].reshape(512, AC), preferred_element_type=F32)

    def act_dot2(hh):
        lhs = jnp.concatenate([act[hh, zz, AY:AR, :] for zz in range(8)], axis=1)
        rhs = jnp.concatenate([ea2[zz, hh] for zz in range(8)], axis=0)
        return jnp.dot(lhs, rhs, preferred_element_type=F32)

    def s_ring(half, hop):
        if hop < 4 or half == 0:
            pos = mod(z - hop + 1, 8)
            send(g_slot(pos, half), g_slot(pos, half), sr_s.at[0, half, hop - 1], sr_r.at[0, half, hop - 1], up)
        if hop < 4 or half == 1:
            pos = mod(z + hop - 1, 8)
            send(g_slot(pos, half), g_slot(pos, half), sr_s.at[1, half, hop - 1], sr_r.at[1, half, hop - 1], down)

    def s_got(half, hop):
        if hop < 4 or half == 0:
            arrived(g_slot(mod(z - hop, 8), half), sr_r.at[0, half, hop - 1])
        if hop < 4 or half == 1:
            arrived(g_slot(mod(z + hop, 8), half), sr_r.at[1, half, hop - 1])

    y_mid(act_y, a_s, a_r)
    y_mid(g_y, s1_s, s1_r)
    y_in(act_y, a_r)
    act_ring(1)
    for j in range(1, 8):
        arrived(act_z(mod(z - j, 8)), az_r.at[j])
    y_out(act_col, c_s, c_r)
    total = act_dot(z)
    y_in(g_y, s1_r)
    s_ring(0, 1)
    s_ring(1, 1)
    act_got(1)
    act_ring(2)
    arrived(sq.at[zr], sq_r.at[7], jnp.logical_and(h != x, za == l))
    for j in range(1, 8):
        send(sq.at[zr], sq.at[zr], sq_s.at[3 + j], sq_r.at[j - 1],
             device(x, l, k, h, mod(z + j, 8)), za == l)
    for j in range(1, 8):
        arrived(g_z(mod(z - j, 8)), gz_r.at[j])
    y_mid(act_col, c_s, c_r)
    y_out(g_col, gc_s, gc_r)
    total += act_dot(mod(z - 1, 8)) + act_dot(mod(z + 1, 8))

    arrived(e_at(x, 1 - l), ex_r.at[0])
    send(e_at(x, 1 - l), e_at(x, 1 - l), ex_s.at[3], ex_r.at[3], right)
    send(e_at(x, 1 - l), e_at(x, 1 - l), ex_s.at[4], ex_r.at[4], left)
    e_pass(x, 1 - l, 1)
    act_got(2)
    act_ring(3)
    total += act_dot(mod(z - 2, 8)) + act_dot(mod(z + 2, 8))

    arrived(e_at(xm, l), ex_r.at[1])
    send(e_at(xm, l, 0), e_at(xm, l, 0), ex_s.at[5], ex_r.at[5], right)
    e_pass(xm, l, 2)
    arrived(e_at(xp, l), ex_r.at[2])
    send(e_at(xp, l, 1), e_at(xp, l, 1), ex_s.at[6], ex_r.at[6], left)
    e_pass(xp, l, 3)

    act_got(3)
    act_ring(4)
    total += act_dot(mod(z - 3, 8)) + act_dot(mod(z + 3, 8))
    total2 = act_dot2(h) + act_dot2(hm) + act_dot2(hp)
    s_got(0, 1)
    s_ring(0, 2)
    s_got(1, 1)
    s_ring(1, 2)
    y_in(act_col, c_r)
    total2 += act_dot2(ho)
    act_got(4)
    total += act_dot(mod(z + 4, 8))
    rab[0:AY, :] = total.astype(BF)
    rab[AY:AR, :] = total2.astype(BF)

    send(rab, rs1.at[h], r0_s, r0_r, partner, swap)

    @pl.when(jnp.logical_not(swap))
    def _():
        rs1[h] = rab[...]

    y_mid(g_col, gc_s, gc_r)
    arrived(e_at(xm, 1 - l), ex_r.at[3])
    send(e_at(xm, 1 - l, 0), e_at(xm, 1 - l, 0), ex_s.at[7], ex_r.at[7], right)
    e_pass(xm, 1 - l, 4)
    arrived(e_at(xp, 1 - l), ex_r.at[4])
    send(e_at(xp, 1 - l, 1), e_at(xp, 1 - l, 1), ex_s.at[8], ex_r.at[8], left)
    e_pass(xp, 1 - l, 5)

    def rs_at(hh, part):
        lo, n = ((0, AR), (0, 80), (80, 64))[0 if part is None else part + 1]
        return rs1.at[hh, pl.ds(lo, n), :]

    arrived(rs1.at[h], r0_r, swap)
    y_out(rs_at, r1_s, r1_r)

    s_got(0, 2)
    s_ring(0, 3)
    s_got(1, 2)
    s_ring(1, 3)
    y_mid(rs_at, r1_s, r1_r)
    y_in(g_col, gc_r)
    y_in(rs_at, r1_r)

    kt = zr // 2
    mine = k == kt

    def ra_block(pos, xx, kk):
        return ra.at[pos // 4, pl.ds(pl.multiple_of(xx * 256 + kk * 128, 128), 128),
                     pl.ds(pl.multiple_of((pos % 2) * 128, 128), 128)]

    def ra_slot(pos, half):
        return ra.at[pos // 4, pl.ds(half * 512, 512), pl.ds(pl.multiple_of((pos % 2) * 128, 128), 128)]

    for j in range(1, 4):
        xt = mod(x + j, 4)
        send(rs1.at[xt, pl.ds(0, TOK), :], ra_block(z, x, k), r2_s.at[j], r2_r.at[j], device(xt, l, k, h, z), mine)
    for j in range(4):
        xt = mod(x + j, 4)
        send(rs1.at[xt, pl.ds(0, TOK), :], ra_block(z, x, k), r2_s.at[4 + j], r2_r.at[4 + j],
             device(xt, l, 1 - k, h, z), jnp.logical_not(mine))

    def raq_slot(pos):
        return raq.at[:, pl.ds(pl.multiple_of((pos % 2) * 128, 128), 128)]

    @pl.when(mine)
    def _():
        a = pltpu.make_async_copy(rs1.at[x, pl.ds(0, TOK), :], ra_block(z, x, k), loc.at[2])
        b = pltpu.make_async_copy(rs1.at[x, pl.ds(TOK, QR), :], raq_slot(z), loc.at[3])
        a.start()
        b.start()
        a.wait()
        b.wait()

    arrived(e_at(xo, l, 0), ex_r.at[5])
    arrived(e_at(xo, l, 1), ex_r.at[6])
    e_pass(xo, l, 6)
    arrived(e_at(xo, 1 - l, 0), ex_r.at[7])
    arrived(e_at(xo, 1 - l, 1), ex_r.at[8])
    e_pass(xo, 1 - l, 7)

    s_got(0, 3)
    s_ring(0, 4)
    s_got(1, 3)
    s_ring(1, 4)

    for j in range(1, 4):
        arrived(ra_block(z, mod(x - j, 4), k), r2_r.at[j], mine)
    for j in range(4):
        arrived(ra_block(z, mod(x - j, 4), 1 - k), r2_r.at[4 + j], mine)

    def held(pos):
        return (pos % 4) // 2 == k

    def r_ring(hop):
        for half in range(2):
            if hop < 4 or half == 0:
                pos = mod(z - hop + 1, 8)
                send(ra_slot(pos, half), ra_slot(pos, half), rr_s.at[0, half, hop - 1], rr_r.at[0, half, hop - 1],
                     up, held(pos))
            if hop < 4 or half == 1:
                pos = mod(z + hop - 1, 8)
                send(ra_slot(pos, half), ra_slot(pos, half), rr_s.at[1, half, hop - 1], rr_r.at[1, half, hop - 1],
                     down, held(pos))

    def r_got(hop):
        for half in range(2):
            if hop < 4 or half == 0:
                pos = mod(z - hop, 8)
                arrived(ra_slot(pos, half), rr_r.at[0, half, hop - 1], held(pos))
            if hop < 4 or half == 1:
                pos = mod(z + hop, 8)
                arrived(ra_slot(pos, half), rr_r.at[1, half, hop - 1], held(pos))

    r_ring(1)
    send(raq_slot(z), raq_slot(z), rk_s.at[0], rk_r.at[0], up, held(z))
    send(raq_slot(z), raq_slot(z), rk_s.at[1], rk_r.at[1], down, held(z))

    e_of = [(x, l), (x, 1 - l), (xm, l), (xp, l), (xm, 1 - l), (xp, 1 - l), (xo, l), (xo, 1 - l)]
    for i, (xx, ll) in enumerate(e_of):
        arrived(ebuf.at[xx * 4 + ll * 2 + 1 - k], ec_r.at[i])
    pair = z // 2
    step = 2 * (z % 2) - 1
    order = [pair, mod(pair + step, 4), mod(pair - step, 4), mod(pair + 2, 4)]

    def s_dot(n):
        out = jnp.zeros((GC, TOK), F32)
        for hh in range(4):
            out += jnp.dot(ebuf[hh * 4 + n], gbuf[hh, pl.ds(2 * n, 2)].reshape(640, TOK),
                           preferred_element_type=F32)
        return out

    acc[...] = s_dot(order[0]) + s_dot(order[1])
    acc[...] += s_dot(order[2])

    for j in range(1, 8):
        from_z = mod(z - j, 8)
        arrived(sq.at[from_z % 4], sq_r.at[j - 1], from_z // 4 == l)
    qpart = jnp.zeros((QR, GC), F32)
    for m in range(2):
        zero = jnp.zeros((QR, 384), F32)
        first = jnp.concatenate([sq[2 * m].astype(F32), zero], axis=1)
        second = jnp.concatenate([sq[2 * m + 1].astype(F32), zero], axis=1)
        both = (first + pltpu.roll(second, GC, 1))[:, 0:640].astype(BF)
        qpart += lax.dot_general(both, ebuf[(x * 4 + l * 2) + m], (((1,), (1,)), ((), ())),
                                 preferred_element_type=F32)
    qpb[chip] = jnp.concatenate([qpart, jnp.zeros((QR, 64), F32)], axis=1)
    for b in range(8):
        send(qpb.at[chip], qpb.at[chip], rq_s.at[b], rq_r.at[chip], device(b % 4, b // 4, k, h, z), chip != b)

    s_got(0, 4)
    s_got(1, 4)
    rgb[...] = (acc[...] + s_dot(order[3])).astype(BF)

    def rg_slot(s):
        return rg.at[:, pl.ds(pl.multiple_of(s * 128, 128), 128)]

    for b in range(8):
        send(rgb, rg_slot(shard), ag_s.at[b], ag_r.at[chip], device(b % 4, b // 4, k, h, z), chip != b)
    send(rgb, rg_slot(shard), fw_s.at[chip], fw_r.at[chip], core)
    own_rg = local(rgb, rg_slot(shard), loc.at[4])

    r_got(1)
    r_ring(2)
    pos = mod(z - 1, 8)
    arrived(raq_slot(pos), rk_r.at[0], held(pos))
    send(raq_slot(pos), raq_slot(pos), rk_s.at[2], rk_r.at[2], up, held(pos))
    pos = mod(z + 1, 8)
    arrived(raq_slot(pos), rk_r.at[1], held(pos))

    r_got(2)
    r_ring(3)
    for b in range(8):
        arrived(rg_slot(2 * b + k), ag_r.at[b], chip != b)
        send(rg_slot(2 * b + k), rg_slot(2 * b + k), fw_s.at[b], fw_r.at[b], core, chip != b)
    r_got(3)
    r_ring(4)
    pos = mod(z - 2, 8)
    arrived(raq_slot(pos), rk_r.at[2], held(pos))
    own_rg.wait()
    for b in range(8):
        arrived(rg_slot(2 * b + 1 - k), fw_r.at[b])
    r_got(4)

    tokens = 0
    for s in range(16):
        tokens = tokens + cnt[s]
    tokens = tokens.astype(F32)
    corr_out[...] = jnp.zeros_like(corr_out)
    row = lax.broadcasted_iota(jnp.int32, (256, 1), 0)

    for c in range(8):
        s = (c % 4) * 4 + (c // 4) * 2
        limit = jnp.where(row < 128, cnt[s], cnt[s + 1] + 128)
        ok = (row < limit).astype(F32)
        a = ra[c // 4, (c % 4) * 256:(c % 4) * 256 + 256, :].astype(F32)
        g = rg[:, c * 256:c * 256 + 256].astype(F32)
        corr_out[...] += jnp.dot((g * g).astype(BF), (a * a * ok).astype(BF), preferred_element_type=F32)
    corr = corr_out[...] / tokens + damping
    corr_out[...] = corr

    for b in range(8):
        arrived(qpb.at[b], rq_r.at[b], chip != b)
    qsum = qpb[0]
    for b in range(1, 8):
        qsum += qpb[b]
    qrows = qsum.astype(BF).astype(F32)
    lane = lax.broadcasted_iota(jnp.int32, (QR, 384), 0)
    of = jnp.zeros((QR, 384), jnp.int32)
    for s in range(QR):
        of = jnp.where(lane == s, qof[s], of)
    for q in range(QUERIES):
        picked = jnp.where(of == q, qrows, 0.0).T.astype(BF)[0:GC, :]
        prod = jnp.dot(picked, raq[...], preferred_element_type=F32)
        wts[q] = (prod / corr_out[...]).astype(BF)

    for c in range(8):
        rac = ra[c // 4, (c % 4) * 256:(c % 4) * 256 + 256, :]
        rgc = rg[:, c * 256:c * 256 + 256].astype(F32)
        rows = []
        for q in range(QUERIES):
            mixed = lax.dot_general(wts[q], rac, (((1,), (1,)), ((), ())), preferred_element_type=F32)
            rows.append(jnp.sum(mixed * rgc, axis=0, keepdims=True))
        fsc[:, c * 256:c * 256 + 256] = jnp.concatenate(rows, axis=0)
        for s in (2 * c, 2 * c + 1):
            send(fsc.at[:, pl.ds(s * 128, 128)], f1.at[shard], f1_s.at[s], f1_r.at[shard],
                 device((s // 2) % 4, s // 8, s % 2, h, z), shard != s)

    f1[shard] = fsc[:, pl.ds(pl.multiple_of(shard * 128, 128), 128)]
    for s in range(16):
        arrived(f1.at[s], f1_r.at[s], shard != s)
    part = f1[0]
    for s in range(1, 16):
        part += f1[s]
    f2[h] = part
    for j in range(1, 4):
        send(f2.at[h], f2.at[h], f2_s.at[j], f2_r.at[j], device(x, l, k, mod(h + j, 4), z))
    for j in range(1, 4):
        arrived(f2.at[mod(h - j, 4)], f2_r.at[j])
    f3[z] = f2[0] + f2[1] + f2[2] + f2[3]
    for j in range(1, 8):
        send(f3.at[z], f3.at[z], f3_s.at[j], f3_r.at[j], device(x, l, k, h, mod(z + j, 8)))
    for j in range(1, 8):
        arrived(f3.at[mod(z - j, 8)], f3_r.at[j])
    done = f3[0]
    for j in range(1, 8):
        done += f3[j]
    t = lax.broadcasted_iota(jnp.int32, (8, 128), 1)
    done = jnp.where(t < cnt[dp], done, 0.0) * (1.0 / math.sqrt(D * FF * QTOK))
    sc_out[...] = pltpu.roll(done, mod(128 - 4 * owner, 128), 1)

    for c, when in pending:
        if when is None:
            c.wait_send()
        else:
            pl.when(when)(functools.partial(lambda c: c.wait_send(), c))


def per_device(train_act, train_grad, query_act, query_grad, query_of, counts, eig_act, eig_grad):
    vm = pl.BlockSpec(memory_space=pltpu.VMEM)
    hb = pl.BlockSpec(memory_space=pltpu.HBM)
    V = pltpu.VMEM
    dma = pltpu.SemaphoreType.DMA
    scratch = [
        pltpu.SMEM((QR,), jnp.int32), pltpu.SMEM((16,), jnp.int32), V((QR, GC), BF), dma((11,)),
        V((4, 8, AR, AC), BF), V((8, 4, AC, AC), BF), V((16, GC, 640), BF),
        V((QR, 384), BF), V((4, 8, GC, TOK), BF), V((4, QR, 384), BF),
        V((GC, TOK), F32), V((8, QR, 384), F32), V((GC, TOK), BF), V((GC, 2048), BF),
        V((AR, AC), BF), V((4, AR, AC), BF), V((2, 1024, 256), BF), V((QR, 256), BF),
        V((QUERIES, GC, 256), BF), V((8, 2048), F32), V((16, 8, 128), F32), V((4, 8, 128), F32), V((8, 8, 128), F32),
    ]
    counts_of = [
        (4,), (4,), (2, 4), (2, 4), (8,), (8,), (9,), (9,), (4,), (4,),
        (8,), (8,), (8,), (8,), (4,), (4,), (4,), (4,),
        (2, 2, 4), (2, 2, 4), (11,), (8,), (8,), (8,), (8,), (8,), (8,), (8,),
        (), (), (4,), (4,), (8,), (8,), (2, 2, 4), (2, 2, 4), (3,), (3,),
        (16,), (16,), (4,), (4,), (8,), (8,), (5,),
    ]
    scratch += [dma(n) if n else dma for n in counts_of]
    scores, corr = pl.pallas_call(
        kernel,
        out_shape=(jax.ShapeDtypeStruct((8, 128), F32), jax.ShapeDtypeStruct((GC, 256), F32)),
        in_specs=[hb] * 8,
        out_specs=(vm, vm),
        scratch_shapes=scratch,
        compiler_params=pltpu.CompilerParams(
            collective_id=0, has_side_effects=True, vmem_limit_bytes=48 * 2**20),
    )(train_act, train_grad.T, query_act, query_grad, query_of, counts, eig_act.reshape(4, 8, AC, AC), eig_grad.T)
    return scores[:, :4], corr.T


def solution(mesh):
    in_specs = (
        P("dp", "owner"),
        P("dp", "owner"),
        P(None, "owner"),
        P(None, "owner"),
        P(),
        P(),
        P(None, "owner"),
        P("dp", "owner"),
    )
    out_specs = (P(None, ("dp", "owner")), P("dp", "owner"))
    return jax.shard_map(
        per_device, mesh=mesh, in_specs=in_specs, out_specs=out_specs, check_vma=False
    )
```

```python
import functools
import math

import jax
import jax.numpy as jnp
from jax import lax
from jax.experimental import pallas as pl
from jax.experimental.pallas import tpu as pltpu
from jax.sharding import PartitionSpec as P

D = 4096
FF = 10240
QUERIES = 8
QTOK = 2
damping = 0.1

MESH = pl.DeviceIdType.MESH
BF = jnp.bfloat16
F32 = jnp.float32

TOK = 128
AC = 128
GC = 320
QR = 16
AR = TOK + QR
AY = 80
GY = 240


def mod(value, size):
    return lax.rem(value + size, size)


def device(x, l, k, h, z):
    return (x * 4 + l * 2 + k, h * 8 + z)


def kernel(ta, tg, qa, qg, qof_in, cnt_in, ea, eg, sc_out, corr_out,
           qof, cnt, qgv, ld, act, ea2, ebuf, qmsg, gbuf, sq, acc, qpb, rgb, rg,
           rab, rs1, ra, raq, wts, fsc, f1, f2, f3, *sems):
    (a_s, a_r, ar_s, ar_r, ec_s, ec_r, ex_s, ex_r, s1_s, s1_r,
     az_s, az_r, gz_s, gz_r, c_s, c_r, gc_s, gc_r,
     sr_s, sr_r, sq_s, sq_r, rq_s, rq_r, ag_s, ag_r, fw_s, fw_r,
     r0_s, r0_r, r1_s, r1_r, r2_s, r2_r, rr_s, rr_r, rk_s, rk_r,
     f1_s, f1_r, f2_s, f2_r, f3_s, f3_r, loc) = sems
    dp, owner = lax.axis_index("dp"), lax.axis_index("owner")
    x, l, k = dp // 4, (dp // 2) % 2, dp % 2
    h, z = owner // 8, owner % 8
    za, zr = z // 4, z % 4
    swap = za != l
    partner = device(x, za, k, h, 4 * l + zr)
    chip = l * 4 + x
    shard = chip * 2 + k
    zp, zm = mod(z + 1, 8), mod(z - 1, 8)
    core = device(x, l, 1 - k, h, z)
    up, down = device(x, l, k, h, zp), device(x, l, k, h, zm)

    pending = []

    def copy(src, dst, ss, rs, to):
        return pltpu.make_async_remote_copy(
            src_ref=src, dst_ref=dst, send_sem=ss, recv_sem=rs, device_id=to, device_id_type=MESH)

    def send(src, dst, ss, rs, to, when=None):
        c = copy(src, dst, ss, rs, to)
        if when is None:
            c.start()
        else:
            pl.when(when)(lambda: c.start())
        pending.append((c, when))

    def arrived(dst, rs, when=None):
        c = copy(dst, dst, rs, rs, core)
        if when is None:
            c.wait_recv()
        else:
            pl.when(when)(lambda: c.wait_recv())

    def flush():
        for c, when in pending:
            if when is None:
                c.wait_send()
            else:
                pl.when(when)(functools.partial(lambda c: c.wait_send(), c))
        pending.clear()

    bar = pltpu.get_barrier_semaphore()
    peers = [device(x, l, k, mod(h + j, 4), z) for j in range(1, 4)]
    peers += [device(x, l, k, h, mod(z + j, 8)) for j in range(1, 8)]

    def plane(s):
        return device((s // 2) % 4, s // 8, s % 2, h, z)

    peers += [plane(mod(shard + j, 16)) for j in range(1, 16)]
    for p in peers:
        pl.semaphore_signal(bar, inc=1, device_id=p, device_id_type=MESH)

    @pl.when(swap)
    def _():
        pl.semaphore_signal(bar, inc=1, device_id=partner, device_id_type=MESH)

    def local(src, dst, sem):
        c = pltpu.make_async_copy(src, dst, sem)
        c.start()
        return c

    loads = [local(ta, act.at[h, z, pl.ds(0, TOK), :], ld.at[0]),
             local(qa, act.at[h, z, pl.ds(TOK, QR), :], ld.at[1]),
             local(qg, qgv, ld.at[2]), local(tg, gbuf.at[h, z], ld.at[3]), local(eg, ebuf.at[dp], ld.at[4]),
             local(qof_in, qof, ld.at[5]), local(cnt_in, cnt, ld.at[6])]
    loads += [local(ea.at[hh], ea2.at[:, hh], ld.at[7 + hh]) for hh in range(4)]
    for c in loads:
        c.wait()
    qmsg[...] = jnp.zeros_like(qmsg)
    qmsg[:, 0:GC] = qgv[...]

    @pl.when(swap)
    def _():
        pl.semaphore_wait(bar, len(peers) + 1)

    @pl.when(jnp.logical_not(swap))
    def _():
        pl.semaphore_wait(bar, len(peers))

    hp, hm, ho = mod(h + 1, 4), mod(h - 1, 4), mod(h + 2, 4)
    above, below = device(x, l, k, hp, z), device(x, l, k, hm, z)

    def y_out(get, ss, rs):
        send(get(h, None), get(h, None), ss.at[0], rs.at[0], above)
        send(get(h, None), get(h, None), ss.at[1], rs.at[1], below)

    def y_mid(get, ss, rs):
        arrived(get(hm, None), rs.at[0])
        send(get(hm, 0), get(hm, 0), ss.at[2], rs.at[2], above)
        arrived(get(hp, None), rs.at[1])
        send(get(hp, 1), get(hp, 1), ss.at[3], rs.at[3], below)

    def y_in(get, rs):
        arrived(get(ho, 0), rs.at[2])
        arrived(get(ho, 1), rs.at[3])

    def act_y(hh, part):
        lo, n = ((0, AY), (0, 48), (48, AY - 48))[0 if part is None else part + 1]
        return act.at[hh, z, pl.ds(lo, n), :]

    def g_y(hh, part):
        lo, n = ((0, GY), (0, 128), (128, GY - 128))[0 if part is None else part + 1]
        return gbuf.at[hh, z, pl.ds(lo, n), :]

    def act_col(hh, part):
        zs = pl.ds(0, 8) if part is None else pl.ds(4 * part, 4)
        return act.at[hh, zs, pl.ds(AY, AR - AY), :]

    def g_col(hh, part):
        zs = pl.ds(0, 8) if part is None else pl.ds(4 * part, 4)
        return gbuf.at[hh, zs, pl.ds(GY, GC - GY), :]

    def act_z(pos):
        return act.at[h, pos, pl.ds(AY, AR - AY), :]

    def g_z(pos):
        return gbuf.at[h, pos, pl.ds(GY, GC - GY), :]

    y_out(act_y, a_s, a_r)
    y_out(g_y, s1_s, s1_r)
    for j in (1, 7, 2, 6, 3, 5, 4):
        send(act_z(z), act_z(z), az_s.at[j], az_r.at[j], device(x, l, k, h, mod(z + j, 8)))
    for j in (1, 7, 2, 6, 3, 5, 4):
        send(g_z(z), g_z(z), gz_s.at[j], gz_r.at[j], device(x, l, k, h, mod(z + j, 8)))

    for j in range(1, 4):
        send(qmsg, sq.at[zr], sq_s.at[j], sq_r.at[7], device(x, l, k, mod(h + j, 4), z),
             jnp.logical_and(h == x, za == l))

    @pl.when(jnp.logical_and(h == x, za == l))
    def _():
        sq[zr] = qmsg[...]

    def e_at(xx, ll, part=None):
        d = xx * 4 + ll * 2 + k
        if part is None:
            return ebuf.at[d]
        return ebuf.at[d, pl.ds(part * 160, 160), :]

    xp, xm, xo = mod(x + 1, 4), mod(x - 1, 4), mod(x + 2, 4)
    right, left = device(xp, l, k, h, z), device(xm, l, k, h, z)
    beside = device(x, 1 - l, k, h, z)

    def e_pass(xx, ll, i):
        send(e_at(xx, ll), e_at(xx, ll), ec_s.at[i], ec_r.at[i], core)

    send(e_at(x, l), e_at(x, l), ex_s.at[0], ex_r.at[0], beside)
    send(e_at(x, l), e_at(x, l), ex_s.at[1], ex_r.at[1], right)
    send(e_at(x, l), e_at(x, l), ex_s.at[2], ex_r.at[2], left)
    e_pass(x, l, 0)

    def act_slot(pos, lo=0, n=4):
        return act.at[pl.ds(lo, n), pos, pl.ds(0, AY), :]

    def g_slot(pos, half):
        return gbuf.at[pl.ds(half * 2, 2), pos, pl.ds(0, GY), :]

    def act_ring(hop):
        n = 4 if hop < 4 else 2
        pos = mod(z - hop + 1, 8)
        send(act_slot(pos, 0, n), act_slot(pos, 0, n), ar_s.at[0, hop - 1], ar_r.at[0, hop - 1], up)
        pos = mod(z + hop - 1, 8)
        lo = 4 - n
        send(act_slot(pos, lo, n), act_slot(pos, lo, n), ar_s.at[1, hop - 1], ar_r.at[1, hop - 1], down)

    def act_got(hop):
        n = 4 if hop < 4 else 2
        arrived(act_slot(mod(z - hop, 8), 0, n), ar_r.at[0, hop - 1])
        arrived(act_slot(mod(z + hop, 8), 4 - n, n), ar_r.at[1, hop - 1])

    def act_dot(pos):
        lhs = jnp.concatenate([act[hh, pos, 0:AY, :] for hh in range(4)], axis=1)
        return jnp.dot(lhs, ea2[pos].reshape(512, AC), preferred_element_type=F32)

    def act_dot2(hh):
        lhs = jnp.concatenate([act[hh, zz, AY:AR, :] for zz in range(8)], axis=1)
        rhs = jnp.concatenate([ea2[zz, hh] for zz in range(8)], axis=0)
        return jnp.dot(lhs, rhs, preferred_element_type=F32)

    def s_ring(half, hop):
        if hop < 4 or half == 0:
            pos = mod(z - hop + 1, 8)
            send(g_slot(pos, half), g_slot(pos, half), sr_s.at[0, half, hop - 1], sr_r.at[0, half, hop - 1], up)
        if hop < 4 or half == 1:
            pos = mod(z + hop - 1, 8)
            send(g_slot(pos, half), g_slot(pos, half), sr_s.at[1, half, hop - 1], sr_r.at[1, half, hop - 1], down)

    def s_got(half, hop):
        if hop < 4 or half == 0:
            arrived(g_slot(mod(z - hop, 8), half), sr_r.at[0, half, hop - 1])
        if hop < 4 or half == 1:
            arrived(g_slot(mod(z + hop, 8), half), sr_r.at[1, half, hop - 1])

    y_mid(act_y, a_s, a_r)
    for j in range(1, 8):
        arrived(act_z(mod(z - j, 8)), az_r.at[j])
    y_out(act_col, c_s, c_r)
    y_mid(g_y, s1_s, s1_r)
    y_in(act_y, a_r)
    act_ring(1)
    y_in(g_y, s1_r)
    s_ring(0, 1)
    s_ring(1, 1)
    for j in range(1, 8):
        arrived(g_z(mod(z - j, 8)), gz_r.at[j])
    y_out(g_col, gc_s, gc_r)
    arrived(sq.at[zr], sq_r.at[7], jnp.logical_and(h != x, za == l))
    for j in range(1, 8):
        send(sq.at[zr], sq.at[zr], sq_s.at[3 + j], sq_r.at[j - 1],
             device(x, l, k, h, mod(z + j, 8)), za == l)
    total = act_dot(z)
    act_got(1)
    act_ring(2)
    total += act_dot(mod(z - 1, 8)) + act_dot(mod(z + 1, 8))

    arrived(e_at(x, 1 - l), ex_r.at[0])
    send(e_at(x, 1 - l), e_at(x, 1 - l), ex_s.at[3], ex_r.at[3], right)
    send(e_at(x, 1 - l), e_at(x, 1 - l), ex_s.at[4], ex_r.at[4], left)
    e_pass(x, 1 - l, 1)
    arrived(e_at(xm, l), ex_r.at[1])
    send(e_at(xm, l, 0), e_at(xm, l, 0), ex_s.at[5], ex_r.at[5], right)
    e_pass(xm, l, 2)
    arrived(e_at(xp, l), ex_r.at[2])
    send(e_at(xp, l, 1), e_at(xp, l, 1), ex_s.at[6], ex_r.at[6], left)
    e_pass(xp, l, 3)
    y_mid(act_col, c_s, c_r)
    act_got(2)
    act_ring(3)
    total2 = act_dot2(h)
    s_got(0, 1)
    s_ring(0, 2)
    s_got(1, 1)
    s_ring(1, 2)
    total += act_dot(mod(z - 2, 8)) + act_dot(mod(z + 2, 8))
    act_got(3)
    act_ring(4)
    y_in(act_col, c_r)
    total += act_dot(mod(z - 3, 8)) + act_dot(mod(z + 3, 8))
    total2 += act_dot2(hm) + act_dot2(hp) + act_dot2(ho)
    act_got(4)
    total += act_dot(mod(z + 4, 8))
    rab[0:AY, :] = total.astype(BF)
    rab[AY:AR, :] = total2.astype(BF)

    send(rab, rs1.at[h], r0_s, r0_r, partner, swap)

    @pl.when(jnp.logical_not(swap))
    def _():
        rs1[h] = rab[...]

    y_mid(g_col, gc_s, gc_r)
    s_got(0, 2)
    s_ring(0, 3)
    s_got(1, 2)
    s_ring(1, 3)

    arrived(rs1.at[h], r0_r, swap)
    for j in range(1, 4):
        send(rs1.at[h], rs1.at[h], r1_s.at[j], r1_r.at[j], device(x, l, k, mod(h + j, 4), z))
    arrived(e_at(xm, 1 - l), ex_r.at[3])
    send(e_at(xm, 1 - l, 0), e_at(xm, 1 - l, 0), ex_s.at[7], ex_r.at[7], right)
    e_pass(xm, 1 - l, 4)
    arrived(e_at(xp, 1 - l), ex_r.at[4])
    send(e_at(xp, 1 - l, 1), e_at(xp, 1 - l, 1), ex_s.at[8], ex_r.at[8], left)
    e_pass(xp, 1 - l, 5)

    for j in range(1, 4):
        arrived(rs1.at[mod(h - j, 4)], r1_r.at[j])
    kt = zr // 2
    mine = k == kt

    def ra_block(pos, xx, kk):
        return ra.at[pos // 4, pl.ds(pl.multiple_of(xx * 256 + kk * 128, 128), 128),
                     pl.ds(pl.multiple_of((pos % 2) * 128, 128), 128)]

    def ra_slot(pos, half):
        return ra.at[pos // 4, pl.ds(half * 512, 512), pl.ds(pl.multiple_of((pos % 2) * 128, 128), 128)]

    for j in range(1, 4):
        xt = mod(x + j, 4)
        send(rs1.at[xt, pl.ds(0, TOK), :], ra_block(z, x, k), r2_s.at[j], r2_r.at[j], device(xt, l, k, h, z), mine)
    for j in range(4):
        xt = mod(x + j, 4)
        send(rs1.at[xt, pl.ds(0, TOK), :], ra_block(z, x, k), r2_s.at[4 + j], r2_r.at[4 + j],
             device(xt, l, 1 - k, h, z), jnp.logical_not(mine))

    def raq_slot(pos):
        return raq.at[:, pl.ds(pl.multiple_of((pos % 2) * 128, 128), 128)]

    @pl.when(mine)
    def _():
        a = pltpu.make_async_copy(rs1.at[x, pl.ds(0, TOK), :], ra_block(z, x, k), loc.at[2])
        b = pltpu.make_async_copy(rs1.at[x, pl.ds(TOK, QR), :], raq_slot(z), loc.at[3])
        a.start()
        b.start()
        a.wait()
        b.wait()

    s_got(0, 3)
    s_ring(0, 4)
    s_got(1, 3)
    s_ring(1, 4)
    arrived(e_at(xo, l, 0), ex_r.at[5])
    arrived(e_at(xo, l, 1), ex_r.at[6])
    e_pass(xo, l, 6)
    for j in range(1, 4):
        arrived(ra_block(z, mod(x - j, 4), k), r2_r.at[j], mine)
    for j in range(4):
        arrived(ra_block(z, mod(x - j, 4), 1 - k), r2_r.at[4 + j], mine)

    def held(pos):
        return (pos % 4) // 2 == k

    def r_ring(hop):
        for half in range(2):
            if hop < 4 or half == 0:
                pos = mod(z - hop + 1, 8)
                send(ra_slot(pos, half), ra_slot(pos, half), rr_s.at[0, half, hop - 1], rr_r.at[0, half, hop - 1],
                     up, held(pos))
            if hop < 4 or half == 1:
                pos = mod(z + hop - 1, 8)
                send(ra_slot(pos, half), ra_slot(pos, half), rr_s.at[1, half, hop - 1], rr_r.at[1, half, hop - 1],
                     down, held(pos))

    def r_got(hop):
        for half in range(2):
            if hop < 4 or half == 0:
                pos = mod(z - hop, 8)
                arrived(ra_slot(pos, half), rr_r.at[0, half, hop - 1], held(pos))
            if hop < 4 or half == 1:
                pos = mod(z + hop, 8)
                arrived(ra_slot(pos, half), rr_r.at[1, half, hop - 1], held(pos))

    r_ring(1)
    send(raq_slot(z), raq_slot(z), rk_s.at[0], rk_r.at[0], up, held(z))
    send(raq_slot(z), raq_slot(z), rk_s.at[1], rk_r.at[1], down, held(z))

    arrived(e_at(xo, 1 - l, 0), ex_r.at[7])
    arrived(e_at(xo, 1 - l, 1), ex_r.at[8])
    e_pass(xo, 1 - l, 7)
    y_in(g_col, gc_r)

    e_of = [(x, l), (x, 1 - l), (xm, l), (xp, l), (xm, 1 - l), (xp, 1 - l), (xo, l), (xo, 1 - l)]
    for i, (xx, ll) in enumerate(e_of):
        arrived(ebuf.at[xx * 4 + ll * 2 + 1 - k], ec_r.at[i])
    pair = z // 2
    step = 2 * (z % 2) - 1
    order = [pair, mod(pair + step, 4), mod(pair - step, 4), mod(pair + 2, 4)]

    def s_dot(n):
        out = jnp.zeros((GC, TOK), F32)
        for hh in range(4):
            out += jnp.dot(ebuf[hh * 4 + n], gbuf[hh, pl.ds(2 * n, 2)].reshape(640, TOK),
                           preferred_element_type=F32)
        return out

    acc[...] = s_dot(order[0]) + s_dot(order[1])
    acc[...] += s_dot(order[2])
    s_got(0, 4)
    s_got(1, 4)
    rgb[...] = (acc[...] + s_dot(order[3])).astype(BF)

    def rg_slot(s):
        return rg.at[:, pl.ds(pl.multiple_of(s * 128, 128), 128)]

    for b in range(8):
        send(rgb, rg_slot(shard), ag_s.at[b], ag_r.at[chip], device(b % 4, b // 4, k, h, z), chip != b)
    send(rgb, rg_slot(shard), fw_s.at[chip], fw_r.at[chip], core)
    own_rg = local(rgb, rg_slot(shard), loc.at[4])

    r_got(1)
    r_ring(2)
    pos = mod(z - 1, 8)
    arrived(raq_slot(pos), rk_r.at[0], held(pos))
    send(raq_slot(pos), raq_slot(pos), rk_s.at[2], rk_r.at[2], up, held(pos))
    pos = mod(z + 1, 8)
    arrived(raq_slot(pos), rk_r.at[1], held(pos))

    for j in range(1, 8):
        from_z = mod(z - j, 8)
        arrived(sq.at[from_z % 4], sq_r.at[j - 1], from_z // 4 == l)
    qpart = jnp.zeros((QR, GC), F32)
    for m in range(2):
        zero = jnp.zeros((QR, 384), F32)
        first = jnp.concatenate([sq[2 * m].astype(F32), zero], axis=1)
        second = jnp.concatenate([sq[2 * m + 1].astype(F32), zero], axis=1)
        both = (first + pltpu.roll(second, GC, 1))[:, 0:640].astype(BF)
        qpart += lax.dot_general(both, ebuf[(x * 4 + l * 2) + m], (((1,), (1,)), ((), ())),
                                 preferred_element_type=F32)
    qpb[chip] = jnp.concatenate([qpart, jnp.zeros((QR, 64), F32)], axis=1)
    for b in range(8):
        send(qpb.at[chip], qpb.at[chip], rq_s.at[b], rq_r.at[chip], device(b % 4, b // 4, k, h, z), chip != b)

    r_got(2)
    r_ring(3)
    for b in range(8):
        arrived(rg_slot(2 * b + k), ag_r.at[b], chip != b)
        send(rg_slot(2 * b + k), rg_slot(2 * b + k), fw_s.at[b], fw_r.at[b], core, chip != b)
    r_got(3)
    r_ring(4)
    pos = mod(z - 2, 8)
    arrived(raq_slot(pos), rk_r.at[2], held(pos))
    own_rg.wait()
    for b in range(8):
        arrived(rg_slot(2 * b + 1 - k), fw_r.at[b])
    r_got(4)

    tokens = 0
    for s in range(16):
        tokens = tokens + cnt[s]
    tokens = tokens.astype(F32)
    corr_out[...] = jnp.zeros_like(corr_out)
    row = lax.broadcasted_iota(jnp.int32, (256, 1), 0)

    for c in range(8):
        s = (c % 4) * 4 + (c // 4) * 2
        limit = jnp.where(row < 128, cnt[s], cnt[s + 1] + 128)
        ok = (row < limit).astype(F32)
        a = ra[c // 4, (c % 4) * 256:(c % 4) * 256 + 256, :].astype(F32)
        g = rg[:, c * 256:c * 256 + 256].astype(F32)
        corr_out[...] += jnp.dot((g * g).astype(BF), (a * a * ok).astype(BF), preferred_element_type=F32)
    corr = corr_out[...] / tokens + damping
    corr_out[...] = corr

    for b in range(8):
        arrived(qpb.at[b], rq_r.at[b], chip != b)
    qsum = qpb[0]
    for b in range(1, 8):
        qsum += qpb[b]
    qrows = qsum.astype(BF).astype(F32)
    lane = lax.broadcasted_iota(jnp.int32, (QR, 384), 0)
    of = jnp.zeros((QR, 384), jnp.int32)
    for s in range(QR):
        of = jnp.where(lane == s, qof[s], of)
    for q in range(QUERIES):
        picked = jnp.where(of == q, qrows, 0.0).T.astype(BF)[0:GC, :]
        prod = jnp.dot(picked, raq[...], preferred_element_type=F32)
        wts[q] = (prod / corr_out[...]).astype(BF)

    for c in range(8):
        rac = ra[c // 4, (c % 4) * 256:(c % 4) * 256 + 256, :]
        rgc = rg[:, c * 256:c * 256 + 256].astype(F32)
        rows = []
        for q in range(QUERIES):
            mixed = lax.dot_general(wts[q], rac, (((1,), (1,)), ((), ())), preferred_element_type=F32)
            rows.append(jnp.sum(mixed * rgc, axis=0, keepdims=True))
        fsc[:, c * 256:c * 256 + 256] = jnp.concatenate(rows, axis=0)
        for s in (2 * c, 2 * c + 1):
            send(fsc.at[:, pl.ds(s * 128, 128)], f1.at[shard], f1_s.at[s], f1_r.at[shard],
                 device((s // 2) % 4, s // 8, s % 2, h, z), shard != s)

    f1[shard] = fsc[:, pl.ds(pl.multiple_of(shard * 128, 128), 128)]
    for s in range(16):
        arrived(f1.at[s], f1_r.at[s], shard != s)
    part = f1[0]
    for s in range(1, 16):
        part += f1[s]
    f2[h] = part
    for j in range(1, 4):
        send(f2.at[h], f2.at[h], f2_s.at[j], f2_r.at[j], device(x, l, k, mod(h + j, 4), z))
    for j in range(1, 4):
        arrived(f2.at[mod(h - j, 4)], f2_r.at[j])
    f3[z] = f2[0] + f2[1] + f2[2] + f2[3]
    for j in range(1, 8):
        send(f3.at[z], f3.at[z], f3_s.at[j], f3_r.at[j], device(x, l, k, h, mod(z + j, 8)))
    for j in range(1, 8):
        arrived(f3.at[mod(z - j, 8)], f3_r.at[j])
    done = f3[0]
    for j in range(1, 8):
        done += f3[j]
    t = lax.broadcasted_iota(jnp.int32, (8, 128), 1)
    done = jnp.where(t < cnt[dp], done, 0.0) * (1.0 / math.sqrt(D * FF * QTOK))
    sc_out[...] = pltpu.roll(done, mod(128 - 4 * owner, 128), 1)

    flush()


def per_device(train_act, train_grad, query_act, query_grad, query_of, counts, eig_act, eig_grad):
    vm = pl.BlockSpec(memory_space=pltpu.VMEM)
    hb = pl.BlockSpec(memory_space=pltpu.HBM)
    V = pltpu.VMEM
    dma = pltpu.SemaphoreType.DMA
    scratch = [
        pltpu.SMEM((QR,), jnp.int32), pltpu.SMEM((16,), jnp.int32), V((QR, GC), BF), dma((11,)),
        V((4, 8, AR, AC), BF), V((8, 4, AC, AC), BF), V((16, GC, 640), BF),
        V((QR, 384), BF), V((4, 8, GC, TOK), BF), V((4, QR, 384), BF),
        V((GC, TOK), F32), V((8, QR, 384), F32), V((GC, TOK), BF), V((GC, 2048), BF),
        V((AR, AC), BF), V((4, AR, AC), BF), V((2, 1024, 256), BF), V((QR, 256), BF),
        V((QUERIES, GC, 256), BF), V((8, 2048), F32), V((16, 8, 128), F32), V((4, 8, 128), F32), V((8, 8, 128), F32),
    ]
    counts_of = [
        (4,), (4,), (2, 4), (2, 4), (8,), (8,), (9,), (9,), (4,), (4,),
        (8,), (8,), (8,), (8,), (4,), (4,), (4,), (4,),
        (2, 2, 4), (2, 2, 4), (11,), (8,), (8,), (8,), (8,), (8,), (8,), (8,),
        (), (), (4,), (4,), (8,), (8,), (2, 2, 4), (2, 2, 4), (3,), (3,),
        (16,), (16,), (4,), (4,), (8,), (8,), (5,),
    ]
    scratch += [dma(n) if n else dma for n in counts_of]
    scores, corr = pl.pallas_call(
        kernel,
        out_shape=(jax.ShapeDtypeStruct((8, 128), F32), jax.ShapeDtypeStruct((GC, 256), F32)),
        in_specs=[hb] * 8,
        out_specs=(vm, vm),
        scratch_shapes=scratch,
        compiler_params=pltpu.CompilerParams(
            collective_id=0, has_side_effects=True, vmem_limit_bytes=60 * 2**20),
    )(train_act, train_grad.T, query_act, query_grad, query_of, counts, eig_act.reshape(4, 8, AC, AC), eig_grad.T)
    return scores[:, :4], corr.T


def solution(mesh):
    in_specs = (
        P("dp", "owner"),
        P("dp", "owner"),
        P(None, "owner"),
        P(None, "owner"),
        P(),
        P(),
        P(None, "owner"),
        P("dp", "owner"),
    )
    out_specs = (P(None, ("dp", "owner")), P("dp", "owner"))
    return jax.shard_map(
        per_device, mesh=mesh, in_specs=in_specs, out_specs=out_specs, check_vma=False
    )
```

```python
import functools
import math

import jax
import jax.numpy as jnp
from jax import lax
from jax.experimental import pallas as pl
from jax.experimental.pallas import tpu as pltpu
from jax.sharding import PartitionSpec as P

D = 4096
FF = 10240
QUERIES = 8
QTOK = 2
damping = 0.1

MESH = pl.DeviceIdType.MESH
BF = jnp.bfloat16
F32 = jnp.float32

TOK = 128
AC = 128
GC = 320
QR = 16
AR = TOK + QR
AY = 80
GY = 160


def mod(value, size):
    return lax.rem(value + size, size)


def device(x, l, k, h, z):
    return (x * 4 + l * 2 + k, h * 8 + z)


def kernel(ta, tg, qa, qg, qof_in, cnt_in, ea, eg, sc_out, corr_out,
           qof, cnt, qgv, ld, act, ea2, ebuf, qmsg, gbuf, sq, acc, qpb, rgb, rg,
           rab, rs1, ra, raq, wts, fsc, f1, f2, f3, *sems):
    (a_s, a_r, ar_s, ar_r, ec_s, ec_r, ex_s, ex_r, s1_s, s1_r,
     az_s, az_r, gz_s, gz_r, c_s, c_r, gc_s, gc_r,
     sr_s, sr_r, sq_s, sq_r, rq_s, rq_r, ag_s, ag_r, fw_s, fw_r,
     r0_s, r0_r, r1_s, r1_r, r2_s, r2_r, rr_s, rr_r, rk_s, rk_r,
     f1_s, f1_r, f2_s, f2_r, f3_s, f3_r, loc) = sems
    dp, owner = lax.axis_index("dp"), lax.axis_index("owner")
    x, l, k = dp // 4, (dp // 2) % 2, dp % 2
    h, z = owner // 8, owner % 8
    za, zr = z // 4, z % 4
    swap = za != l
    partner = device(x, za, k, h, 4 * l + zr)
    chip = l * 4 + x
    shard = chip * 2 + k
    zp, zm = mod(z + 1, 8), mod(z - 1, 8)
    core = device(x, l, 1 - k, h, z)
    up, down = device(x, l, k, h, zp), device(x, l, k, h, zm)

    pending = []

    def copy(src, dst, ss, rs, to):
        return pltpu.make_async_remote_copy(
            src_ref=src, dst_ref=dst, send_sem=ss, recv_sem=rs, device_id=to, device_id_type=MESH)

    def send(src, dst, ss, rs, to, when=None):
        c = copy(src, dst, ss, rs, to)
        if when is None:
            c.start()
        else:
            pl.when(when)(lambda: c.start())
        pending.append((c, when))

    def arrived(dst, rs, when=None):
        c = copy(dst, dst, rs, rs, core)
        if when is None:
            c.wait_recv()
        else:
            pl.when(when)(lambda: c.wait_recv())

    def flush():
        for c, when in pending:
            if when is None:
                c.wait_send()
            else:
                pl.when(when)(functools.partial(lambda c: c.wait_send(), c))
        pending.clear()

    bar = pltpu.get_barrier_semaphore()
    peers = [device(x, l, k, mod(h + j, 4), z) for j in range(1, 4)]
    peers += [device(x, l, k, h, mod(z + j, 8)) for j in range(1, 8)]

    def plane(s):
        return device((s // 2) % 4, s // 8, s % 2, h, z)

    peers += [plane(mod(shard + j, 16)) for j in range(1, 16)]
    for p in peers:
        pl.semaphore_signal(bar, inc=1, device_id=p, device_id_type=MESH)

    @pl.when(swap)
    def _():
        pl.semaphore_signal(bar, inc=1, device_id=partner, device_id_type=MESH)

    def local(src, dst, sem):
        c = pltpu.make_async_copy(src, dst, sem)
        c.start()
        return c

    loads = [local(ta, act.at[h, z, pl.ds(0, TOK), :], ld.at[0]),
             local(qa, act.at[h, z, pl.ds(TOK, QR), :], ld.at[1]),
             local(qg, qgv, ld.at[2]), local(tg, gbuf.at[h, z], ld.at[3]), local(eg, ebuf.at[dp], ld.at[4]),
             local(qof_in, qof, ld.at[5]), local(cnt_in, cnt, ld.at[6])]
    loads += [local(ea.at[hh], ea2.at[:, hh], ld.at[7 + hh]) for hh in range(4)]
    for c in loads:
        c.wait()
    qmsg[...] = jnp.zeros_like(qmsg)
    qmsg[:, 0:GC] = qgv[...]

    @pl.when(swap)
    def _():
        pl.semaphore_wait(bar, len(peers) + 1)

    @pl.when(jnp.logical_not(swap))
    def _():
        pl.semaphore_wait(bar, len(peers))

    hp, hm, ho = mod(h + 1, 4), mod(h - 1, 4), mod(h + 2, 4)
    above, below = device(x, l, k, hp, z), device(x, l, k, hm, z)

    def y_out(get, ss, rs):
        send(get(h, None), get(h, None), ss.at[0], rs.at[0], above)
        send(get(h, None), get(h, None), ss.at[1], rs.at[1], below)

    def y_mid(get, ss, rs):
        arrived(get(hm, None), rs.at[0])
        send(get(hm, 0), get(hm, 0), ss.at[2], rs.at[2], above)
        arrived(get(hp, None), rs.at[1])
        send(get(hp, 1), get(hp, 1), ss.at[3], rs.at[3], below)

    def y_in(get, rs):
        arrived(get(ho, 0), rs.at[2])
        arrived(get(ho, 1), rs.at[3])

    def act_y(hh, part):
        lo, n = ((0, AY), (0, 48), (48, AY - 48))[0 if part is None else part + 1]
        return act.at[hh, z, pl.ds(lo, n), :]

    def g_y(hh, part):
        lo, n = ((0, GY), (0, 80), (80, GY - 80))[0 if part is None else part + 1]
        return gbuf.at[hh, z, pl.ds(lo, n), :]

    def act_col(hh, part):
        zs = pl.ds(0, 8) if part is None else pl.ds(4 * part, 4)
        return act.at[hh, zs, pl.ds(AY, AR - AY), :]

    def g_col(hh, part):
        zs = pl.ds(0, 8) if part is None else pl.ds(4 * part, 4)
        return gbuf.at[hh, zs, pl.ds(GY, GC - GY), :]

    def act_z(pos):
        return act.at[h, pos, pl.ds(AY, AR - AY), :]

    def g_z(pos):
        return gbuf.at[h, pos, pl.ds(GY, GC - GY), :]

    y_out(act_y, a_s, a_r)
    y_out(g_y, s1_s, s1_r)
    for j in (1, 7, 2, 6, 3, 5, 4):
        send(act_z(z), act_z(z), az_s.at[j], az_r.at[j], device(x, l, k, h, mod(z + j, 8)))
    for j in (1, 7, 2, 6, 3, 5, 4):
        send(g_z(z), g_z(z), gz_s.at[j], gz_r.at[j], device(x, l, k, h, mod(z + j, 8)))

    for j in range(1, 4):
        send(qmsg, sq.at[zr], sq_s.at[j], sq_r.at[7], device(x, l, k, mod(h + j, 4), z),
             jnp.logical_and(h == x, za == l))

    @pl.when(jnp.logical_and(h == x, za == l))
    def _():
        sq[zr] = qmsg[...]

    def e_at(xx, ll, part=None):
        d = xx * 4 + ll * 2 + k
        if part is None:
            return ebuf.at[d]
        return ebuf.at[d, pl.ds(part * 160, 160), :]

    xp, xm, xo = mod(x + 1, 4), mod(x - 1, 4), mod(x + 2, 4)
    right, left = device(xp, l, k, h, z), device(xm, l, k, h, z)
    beside = device(x, 1 - l, k, h, z)

    def e_pass(xx, ll, i):
        send(e_at(xx, ll), e_at(xx, ll), ec_s.at[i], ec_r.at[i], core)

    send(e_at(x, l), e_at(x, l), ex_s.at[0], ex_r.at[0], beside)
    send(e_at(x, l), e_at(x, l), ex_s.at[1], ex_r.at[1], right)
    send(e_at(x, l), e_at(x, l), ex_s.at[2], ex_r.at[2], left)
    e_pass(x, l, 0)

    def act_slot(pos, lo=0, n=4):
        return act.at[pl.ds(lo, n), pos, pl.ds(0, AY), :]

    def g_slot(pos, half):
        return gbuf.at[pl.ds(half * 2, 2), pos, pl.ds(0, GY), :]

    def act_ring(hop):
        n = 4 if hop < 4 else 2
        pos = mod(z - hop + 1, 8)
        send(act_slot(pos, 0, n), act_slot(pos, 0, n), ar_s.at[0, hop - 1], ar_r.at[0, hop - 1], up)
        pos = mod(z + hop - 1, 8)
        lo = 4 - n
        send(act_slot(pos, lo, n), act_slot(pos, lo, n), ar_s.at[1, hop - 1], ar_r.at[1, hop - 1], down)

    def act_got(hop):
        n = 4 if hop < 4 else 2
        arrived(act_slot(mod(z - hop, 8), 0, n), ar_r.at[0, hop - 1])
        arrived(act_slot(mod(z + hop, 8), 4 - n, n), ar_r.at[1, hop - 1])

    def act_dot(pos):
        lhs = jnp.concatenate([act[hh, pos, 0:AY, :] for hh in range(4)], axis=1)
        return jnp.dot(lhs, ea2[pos].reshape(512, AC), preferred_element_type=F32)

    def act_dot2(hh):
        lhs = jnp.concatenate([act[hh, zz, AY:AR, :] for zz in range(8)], axis=1)
        rhs = jnp.concatenate([ea2[zz, hh] for zz in range(8)], axis=0)
        return jnp.dot(lhs, rhs, preferred_element_type=F32)

    def s_ring(half, hop):
        if hop < 4 or half == 0:
            pos = mod(z - hop + 1, 8)
            send(g_slot(pos, half), g_slot(pos, half), sr_s.at[0, half, hop - 1], sr_r.at[0, half, hop - 1], up)
        if hop < 4 or half == 1:
            pos = mod(z + hop - 1, 8)
            send(g_slot(pos, half), g_slot(pos, half), sr_s.at[1, half, hop - 1], sr_r.at[1, half, hop - 1], down)

    def s_got(half, hop):
        if hop < 4 or half == 0:
            arrived(g_slot(mod(z - hop, 8), half), sr_r.at[0, half, hop - 1])
        if hop < 4 or half == 1:
            arrived(g_slot(mod(z + hop, 8), half), sr_r.at[1, half, hop - 1])

    y_mid(act_y, a_s, a_r)
    for j in range(1, 8):
        arrived(act_z(mod(z - j, 8)), az_r.at[j])
    y_out(act_col, c_s, c_r)
    y_mid(g_y, s1_s, s1_r)
    y_in(act_y, a_r)
    act_ring(1)
    y_in(g_y, s1_r)
    s_ring(0, 1)
    s_ring(1, 1)
    for j in range(1, 8):
        arrived(g_z(mod(z - j, 8)), gz_r.at[j])
    y_out(g_col, gc_s, gc_r)
    arrived(sq.at[zr], sq_r.at[7], jnp.logical_and(h != x, za == l))
    for j in range(1, 8):
        send(sq.at[zr], sq.at[zr], sq_s.at[3 + j], sq_r.at[j - 1],
             device(x, l, k, h, mod(z + j, 8)), za == l)
    total = act_dot(z)
    act_got(1)
    act_ring(2)
    total += act_dot(mod(z - 1, 8)) + act_dot(mod(z + 1, 8))

    arrived(e_at(x, 1 - l), ex_r.at[0])
    send(e_at(x, 1 - l), e_at(x, 1 - l), ex_s.at[3], ex_r.at[3], right)
    send(e_at(x, 1 - l), e_at(x, 1 - l), ex_s.at[4], ex_r.at[4], left)
    e_pass(x, 1 - l, 1)
    arrived(e_at(xm, l), ex_r.at[1])
    send(e_at(xm, l, 0), e_at(xm, l, 0), ex_s.at[5], ex_r.at[5], right)
    e_pass(xm, l, 2)
    arrived(e_at(xp, l), ex_r.at[2])
    send(e_at(xp, l, 1), e_at(xp, l, 1), ex_s.at[6], ex_r.at[6], left)
    e_pass(xp, l, 3)
    y_mid(act_col, c_s, c_r)
    act_got(2)
    act_ring(3)
    total2 = act_dot2(h)
    s_got(0, 1)
    s_ring(0, 2)
    s_got(1, 1)
    s_ring(1, 2)
    total += act_dot(mod(z - 2, 8)) + act_dot(mod(z + 2, 8))
    act_got(3)
    act_ring(4)
    y_in(act_col, c_r)
    total += act_dot(mod(z - 3, 8)) + act_dot(mod(z + 3, 8))
    total2 += act_dot2(hm) + act_dot2(hp) + act_dot2(ho)
    act_got(4)
    total += act_dot(mod(z + 4, 8))
    rab[0:AY, :] = total.astype(BF)
    rab[AY:AR, :] = total2.astype(BF)

    send(rab, rs1.at[h], r0_s, r0_r, partner, swap)

    @pl.when(jnp.logical_not(swap))
    def _():
        rs1[h] = rab[...]

    y_mid(g_col, gc_s, gc_r)
    s_got(0, 2)
    s_ring(0, 3)
    s_got(1, 2)
    s_ring(1, 3)

    arrived(rs1.at[h], r0_r, swap)
    for j in range(1, 4):
        send(rs1.at[h], rs1.at[h], r1_s.at[j], r1_r.at[j], device(x, l, k, mod(h + j, 4), z))
    arrived(e_at(xm, 1 - l), ex_r.at[3])
    send(e_at(xm, 1 - l, 0), e_at(xm, 1 - l, 0), ex_s.at[7], ex_r.at[7], right)
    e_pass(xm, 1 - l, 4)
    arrived(e_at(xp, 1 - l), ex_r.at[4])
    send(e_at(xp, 1 - l, 1), e_at(xp, 1 - l, 1), ex_s.at[8], ex_r.at[8], left)
    e_pass(xp, 1 - l, 5)

    for j in range(1, 4):
        arrived(rs1.at[mod(h - j, 4)], r1_r.at[j])
    kt = zr // 2
    mine = k == kt

    def ra_block(pos, xx, kk):
        return ra.at[pos // 4, pl.ds(pl.multiple_of(xx * 256 + kk * 128, 128), 128),
                     pl.ds(pl.multiple_of((pos % 2) * 128, 128), 128)]

    def ra_slot(pos, half):
        return ra.at[pos // 4, pl.ds(half * 512, 512), pl.ds(pl.multiple_of((pos % 2) * 128, 128), 128)]

    for j in range(1, 4):
        xt = mod(x + j, 4)
        send(rs1.at[xt, pl.ds(0, TOK), :], ra_block(z, x, k), r2_s.at[j], r2_r.at[j], device(xt, l, k, h, z), mine)
    for j in range(4):
        xt = mod(x + j, 4)
        send(rs1.at[xt, pl.ds(0, TOK), :], ra_block(z, x, k), r2_s.at[4 + j], r2_r.at[4 + j],
             device(xt, l, 1 - k, h, z), jnp.logical_not(mine))

    def raq_slot(pos):
        return raq.at[:, pl.ds(pl.multiple_of((pos % 2) * 128, 128), 128)]

    @pl.when(mine)
    def _():
        a = pltpu.make_async_copy(rs1.at[x, pl.ds(0, TOK), :], ra_block(z, x, k), loc.at[2])
        b = pltpu.make_async_copy(rs1.at[x, pl.ds(TOK, QR), :], raq_slot(z), loc.at[3])
        a.start()
        b.start()
        a.wait()
        b.wait()

    s_got(0, 3)
    s_ring(0, 4)
    s_got(1, 3)
    s_ring(1, 4)
    arrived(e_at(xo, l, 0), ex_r.at[5])
    arrived(e_at(xo, l, 1), ex_r.at[6])
    e_pass(xo, l, 6)
    for j in range(1, 4):
        arrived(ra_block(z, mod(x - j, 4), k), r2_r.at[j], mine)
    for j in range(4):
        arrived(ra_block(z, mod(x - j, 4), 1 - k), r2_r.at[4 + j], mine)

    def held(pos):
        return (pos % 4) // 2 == k

    def r_ring(hop, half):
        if hop < 4 or half == 0:
            pos = mod(z - hop + 1, 8)
            send(ra_slot(pos, half), ra_slot(pos, half), rr_s.at[0, half, hop - 1], rr_r.at[0, half, hop - 1],
                 up, held(pos))
        if hop < 4 or half == 1:
            pos = mod(z + hop - 1, 8)
            send(ra_slot(pos, half), ra_slot(pos, half), rr_s.at[1, half, hop - 1], rr_r.at[1, half, hop - 1],
                 down, held(pos))

    def r_got(hop, half):
        if hop < 4 or half == 0:
            pos = mod(z - hop, 8)
            arrived(ra_slot(pos, half), rr_r.at[0, half, hop - 1], held(pos))
        if hop < 4 or half == 1:
            pos = mod(z + hop, 8)
            arrived(ra_slot(pos, half), rr_r.at[1, half, hop - 1], held(pos))

    def r_step(hop):
        for half in range(2):
            r_got(hop, half)
            if hop < 4:
                r_ring(hop + 1, half)

    r_ring(1, 0)
    r_ring(1, 1)
    send(raq_slot(z), raq_slot(z), rk_s.at[0], rk_r.at[0], up, held(z))
    send(raq_slot(z), raq_slot(z), rk_s.at[1], rk_r.at[1], down, held(z))

    arrived(e_at(xo, 1 - l, 0), ex_r.at[7])
    arrived(e_at(xo, 1 - l, 1), ex_r.at[8])
    e_pass(xo, 1 - l, 7)
    y_in(g_col, gc_r)

    e_of = [(x, l), (x, 1 - l), (xm, l), (xp, l), (xm, 1 - l), (xp, 1 - l), (xo, l), (xo, 1 - l)]
    for i, (xx, ll) in enumerate(e_of):
        arrived(ebuf.at[xx * 4 + ll * 2 + 1 - k], ec_r.at[i])
    pair = z // 2
    step = 2 * (z % 2) - 1
    order = [pair, mod(pair + step, 4), mod(pair - step, 4), mod(pair + 2, 4)]

    def s_dot(n):
        out = jnp.zeros((GC, TOK), F32)
        for hh in range(4):
            out += jnp.dot(ebuf[hh * 4 + n], gbuf[hh, pl.ds(2 * n, 2)].reshape(640, TOK),
                           preferred_element_type=F32)
        return out

    acc[...] = s_dot(order[0]) + s_dot(order[1])
    acc[...] += s_dot(order[2])
    s_got(0, 4)
    s_got(1, 4)
    rgb[...] = (acc[...] + s_dot(order[3])).astype(BF)

    def rg_at(xx, ll, part=None, kk=k):
        lanes = pl.ds(pl.multiple_of(((ll * 4 + xx) * 2 + kk) * 128, 128), 128)
        if part is None:
            return rg.at[:, lanes]
        return rg.at[pl.ds(part * 160, 160), lanes]

    def rg_pass(xx, ll, i, src=None):
        send(rg_at(xx, ll) if src is None else src, rg_at(xx, ll), fw_s.at[i], fw_r.at[i], core)

    send(rgb, rg_at(x, l), ag_s.at[0], ag_r.at[0], beside)
    send(rgb, rg_at(x, l), ag_s.at[1], ag_r.at[1], right)
    send(rgb, rg_at(x, l), ag_s.at[2], ag_r.at[2], left)
    rg_pass(x, l, 0, rgb)
    own_rg = local(rgb, rg_at(x, l), loc.at[4])

    r_step(1)
    pos = mod(z - 1, 8)
    arrived(raq_slot(pos), rk_r.at[0], held(pos))
    send(raq_slot(pos), raq_slot(pos), rk_s.at[2], rk_r.at[2], up, held(pos))
    pos = mod(z + 1, 8)
    arrived(raq_slot(pos), rk_r.at[1], held(pos))

    for j in range(1, 8):
        from_z = mod(z - j, 8)
        arrived(sq.at[from_z % 4], sq_r.at[j - 1], from_z // 4 == l)
    qpart = jnp.zeros((QR, GC), F32)
    for m in range(2):
        zero = jnp.zeros((QR, 384), F32)
        first = jnp.concatenate([sq[2 * m].astype(F32), zero], axis=1)
        second = jnp.concatenate([sq[2 * m + 1].astype(F32), zero], axis=1)
        both = (first + pltpu.roll(second, GC, 1))[:, 0:640].astype(BF)
        qpart += lax.dot_general(both, ebuf[(x * 4 + l * 2) + m], (((1,), (1,)), ((), ())),
                                 preferred_element_type=F32)
    qpb[chip] = jnp.concatenate([qpart, jnp.zeros((QR, 64), F32)], axis=1)
    for b in range(8):
        send(qpb.at[chip], qpb.at[chip], rq_s.at[b], rq_r.at[chip], device(b % 4, b // 4, k, h, z), chip != b)

    arrived(rg_at(x, 1 - l), ag_r.at[0])
    send(rg_at(x, 1 - l), rg_at(x, 1 - l), ag_s.at[3], ag_r.at[3], right)
    send(rg_at(x, 1 - l), rg_at(x, 1 - l), ag_s.at[4], ag_r.at[4], left)
    rg_pass(x, 1 - l, 1)
    arrived(rg_at(xm, l), ag_r.at[1])
    send(rg_at(xm, l, 0), rg_at(xm, l, 0), ag_s.at[5], ag_r.at[5], right)
    rg_pass(xm, l, 2)
    arrived(rg_at(xp, l), ag_r.at[2])
    send(rg_at(xp, l, 1), rg_at(xp, l, 1), ag_s.at[6], ag_r.at[6], left)
    rg_pass(xp, l, 3)
    r_step(2)
    arrived(rg_at(xm, 1 - l), ag_r.at[3])
    send(rg_at(xm, 1 - l, 0), rg_at(xm, 1 - l, 0), ag_s.at[7], ag_r.at[7], right)
    rg_pass(xm, 1 - l, 4)
    arrived(rg_at(xp, 1 - l), ag_r.at[4])
    send(rg_at(xp, 1 - l, 1), rg_at(xp, 1 - l, 1), ag_s.at[8], ag_r.at[8], left)
    rg_pass(xp, 1 - l, 5)
    r_step(3)
    arrived(rg_at(xo, l, 0), ag_r.at[5])
    arrived(rg_at(xo, l, 1), ag_r.at[6])
    rg_pass(xo, l, 6)
    arrived(rg_at(xo, 1 - l, 0), ag_r.at[7])
    arrived(rg_at(xo, 1 - l, 1), ag_r.at[8])
    rg_pass(xo, 1 - l, 7)
    pos = mod(z - 2, 8)
    arrived(raq_slot(pos), rk_r.at[2], held(pos))
    own_rg.wait()
    for i, (xx, ll) in enumerate(e_of):
        arrived(rg_at(xx, ll, None, 1 - k), fw_r.at[i])
    r_step(4)

    tokens = 0
    for s in range(16):
        tokens = tokens + cnt[s]
    tokens = tokens.astype(F32)
    corr_out[...] = jnp.zeros_like(corr_out)
    row = lax.broadcasted_iota(jnp.int32, (256, 1), 0)

    for c in range(8):
        s = (c % 4) * 4 + (c // 4) * 2
        limit = jnp.where(row < 128, cnt[s], cnt[s + 1] + 128)
        ok = (row < limit).astype(F32)
        a = ra[c // 4, (c % 4) * 256:(c % 4) * 256 + 256, :].astype(F32)
        g = rg[:, c * 256:c * 256 + 256].astype(F32)
        corr_out[...] += jnp.dot((g * g).astype(BF), (a * a * ok).astype(BF), preferred_element_type=F32)
    corr = corr_out[...] / tokens + damping
    corr_out[...] = corr

    for b in range(8):
        arrived(qpb.at[b], rq_r.at[b], chip != b)
    qsum = qpb[0]
    for b in range(1, 8):
        qsum += qpb[b]
    qrows = qsum.astype(BF).astype(F32)
    lane = lax.broadcasted_iota(jnp.int32, (QR, 384), 0)
    of = jnp.zeros((QR, 384), jnp.int32)
    for s in range(QR):
        of = jnp.where(lane == s, qof[s], of)
    for q in range(QUERIES):
        picked = jnp.where(of == q, qrows, 0.0).T.astype(BF)[0:GC, :]
        prod = jnp.dot(picked, raq[...], preferred_element_type=F32)
        wts[q] = (prod / corr_out[...]).astype(BF)

    for c in range(8):
        rac = ra[c // 4, (c % 4) * 256:(c % 4) * 256 + 256, :]
        rgc = rg[:, c * 256:c * 256 + 256].astype(F32)
        rows = []
        for q in range(QUERIES):
            mixed = lax.dot_general(wts[q], rac, (((1,), (1,)), ((), ())), preferred_element_type=F32)
            rows.append(jnp.sum(mixed * rgc, axis=0, keepdims=True))
        fsc[:, c * 256:c * 256 + 256] = jnp.concatenate(rows, axis=0)
        for s in (2 * c, 2 * c + 1):
            send(fsc.at[:, pl.ds(s * 128, 128)], f1.at[shard], f1_s.at[s], f1_r.at[shard],
                 device((s // 2) % 4, s // 8, s % 2, h, z), shard != s)

    f1[shard] = fsc[:, pl.ds(pl.multiple_of(shard * 128, 128), 128)]
    for s in range(16):
        arrived(f1.at[s], f1_r.at[s], shard != s)
    part = f1[0]
    for s in range(1, 16):
        part += f1[s]
    f2[h] = part
    for j in range(1, 4):
        send(f2.at[h], f2.at[h], f2_s.at[j], f2_r.at[j], device(x, l, k, mod(h + j, 4), z))
    for j in range(1, 4):
        arrived(f2.at[mod(h - j, 4)], f2_r.at[j])
    f3[z] = f2[0] + f2[1] + f2[2] + f2[3]
    for j in range(1, 8):
        send(f3.at[z], f3.at[z], f3_s.at[j], f3_r.at[j], device(x, l, k, h, mod(z + j, 8)))
    for j in range(1, 8):
        arrived(f3.at[mod(z - j, 8)], f3_r.at[j])
    done = f3[0]
    for j in range(1, 8):
        done += f3[j]
    t = lax.broadcasted_iota(jnp.int32, (8, 128), 1)
    done = jnp.where(t < cnt[dp], done, 0.0) * (1.0 / math.sqrt(D * FF * QTOK))
    sc_out[...] = pltpu.roll(done, mod(128 - 4 * owner, 128), 1)

    flush()


def per_device(train_act, train_grad, query_act, query_grad, query_of, counts, eig_act, eig_grad):
    vm = pl.BlockSpec(memory_space=pltpu.VMEM)
    hb = pl.BlockSpec(memory_space=pltpu.HBM)
    V = pltpu.VMEM
    dma = pltpu.SemaphoreType.DMA
    scratch = [
        pltpu.SMEM((QR,), jnp.int32), pltpu.SMEM((16,), jnp.int32), V((QR, GC), BF), dma((11,)),
        V((4, 8, AR, AC), BF), V((8, 4, AC, AC), BF), V((16, GC, 640), BF),
        V((QR, 384), BF), V((4, 8, GC, TOK), BF), V((4, QR, 384), BF),
        V((GC, TOK), F32), V((8, QR, 384), F32), V((GC, TOK), BF), V((GC, 2048), BF),
        V((AR, AC), BF), V((4, AR, AC), BF), V((2, 1024, 256), BF), V((QR, 256), BF),
        V((QUERIES, GC, 256), BF), V((8, 2048), F32), V((16, 8, 128), F32), V((4, 8, 128), F32), V((8, 8, 128), F32),
    ]
    counts_of = [
        (4,), (4,), (2, 4), (2, 4), (8,), (8,), (9,), (9,), (4,), (4,),
        (8,), (8,), (8,), (8,), (4,), (4,), (4,), (4,),
        (2, 2, 4), (2, 2, 4), (11,), (8,), (8,), (8,), (9,), (9,), (8,), (8,),
        (), (), (4,), (4,), (8,), (8,), (2, 2, 4), (2, 2, 4), (3,), (3,),
        (16,), (16,), (4,), (4,), (8,), (8,), (5,),
    ]
    scratch += [dma(n) if n else dma for n in counts_of]
    scores, corr = pl.pallas_call(
        kernel,
        out_shape=(jax.ShapeDtypeStruct((8, 128), F32), jax.ShapeDtypeStruct((GC, 256), F32)),
        in_specs=[hb] * 8,
        out_specs=(vm, vm),
        scratch_shapes=scratch,
        compiler_params=pltpu.CompilerParams(
            collective_id=0, has_side_effects=True, vmem_limit_bytes=60 * 2**20),
    )(train_act, train_grad.T, query_act, query_grad, query_of, counts, eig_act.reshape(4, 8, AC, AC), eig_grad.T)
    return scores[:, :4], corr.T


def solution(mesh):
    in_specs = (
        P("dp", "owner"),
        P("dp", "owner"),
        P(None, "owner"),
        P(None, "owner"),
        P(),
        P(),
        P(None, "owner"),
        P("dp", "owner"),
    )
    out_specs = (P(None, ("dp", "owner")), P("dp", "owner"))
    return jax.shard_map(
        per_device, mesh=mesh, in_specs=in_specs, out_specs=out_specs, check_vma=False
    )
```
